128 devices in a mesh: layer: 4 (over y), grid: 32 (over x, z, core).
Axes of the slice: x: 4, y: 4, z: 4, core: 2. Of those that a mesh axis runs over, the one named last changes fastest.
Arguments:
- leaf_inverse: float32 [4, 32, 4, 128, 128], P('layer', 'grid'), may hold values from -1 to 2
- leaf_coupling: float32 [4, 32, 4, 128, 128], P('layer', 'grid'), may hold values from -0.5 to 0.5
- leaf_rhs: float32 [4, 32, 4, 128, 128], P('layer', 'grid'), may hold values from -6 to 6
- mid_inverse: float32 [4, 32, 2, 128, 128], P('layer', 'grid'), may hold values from -1 to 2
- mid_coupling: float32 [4, 32, 2, 128, 128], P('layer', 'grid'), may hold values from -0.375 to 0.375
- mid_rhs: float32 [4, 32, 2, 128, 128], P('layer', 'grid'), may hold values from -6 to 6
- mid_top: float32 [4, 32, 2, 4096, 128], P('layer', 'grid'), may hold values from -0.0546875 to 0.0546875
- root_inverse: float32 [4, 32, 128, 128], P('layer', 'grid'), may hold values from -1 to 2
- root_top: float32 [4, 32, 4096, 128], P('layer', 'grid'), may hold values from -0.0546875 to 0.0546875
- root_rhs: float32 [4, 32, 128, 128], P('layer', 'grid'), may hold values from -6 to 6
- top_inverse: float32 [32, 128, 128], P('grid'), may hold values from -1 to 2
- top_factor: float32 [32, 128, 4096], P('grid'), may hold values from -0.25 to 0.25
- top_rhs: float32 [32, 128, 128], P('grid'), may hold values from -6 to 6
- top_pattern: int32 [32, 32], P('grid'), may hold values from 0 to 1, as said below
Outputs:
- leaf_solution: float32 [4, 32, 4, 128, 128], P('layer', 'grid')
- mid_solution: float32 [4, 32, 2, 128, 128], P('layer', 'grid')
- root_solution: float32 [4, 32, 128, 128], P('layer', 'grid')
- top_solution: float32 [32, 128, 128], P('grid')
The draws below stay inside these ranges and needn't reach their ends.
Inputs may be any that keep to these rules, and one draw needn't show every extreme that they name: `top_pattern`: entries (i, j) with j // 4 >= i // 4 are not read; entry (i, 0) is 1 for every i >= 4.
All inputs are finite; a program needn't handle non-finite values.
Results may differ from the reference program's by a relative error of at most 0.00011.
Values sent between devices are 32-bit elements; how exact they have to be, the bound alone decides.
No kernel may reach another device: no remote copies, remote signals or barrier semaphores. Data moves between devices by JAX's collectives and lax.ppermute only.
A program may use at most 64 MiB of HBM per device.

```python
import math
import jax
import jax.numpy as jnp
from jax import lax

BLOCK = 128
NRHS = 128
MIDS = 2
SPAN = 4
LEAVES = 4
LAYERS = 4
GROUP = 32
KTOP = 32


def inverse_blocks(key, dims_shape):
    key_off = jax.random.fold_in(key, 0)
    block_width = dims_shape[-1]
    identity = jnp.eye(block_width, dtype=jnp.float32)
    offdiag_part = 0.35 * jax.random.normal(key_off, dims_shape, jnp.float32) / math.sqrt(block_width)
    diagonal_part = jnp.full(dims_shape[:-1], 0.7, jnp.float32)
    return offdiag_part + identity * diagonal_part[..., None]


def draw_leaf_inverse(key, part):
    return inverse_blocks(key, (LAYERS, GROUP, LEAVES, BLOCK, BLOCK))


def draw_mid_inverse(key, part):
    return inverse_blocks(key, (LAYERS, GROUP, MIDS, BLOCK, BLOCK))


def draw_root_inverse(key, part):
    return inverse_blocks(key, (LAYERS, GROUP, BLOCK, BLOCK))


def draw_top_inverse(key, part):
    return inverse_blocks(key, (KTOP, BLOCK, BLOCK))


def draw_top_pattern(key, part):
    random_bits = jax.random.randint(jax.random.fold_in(key, 17), (KTOP, KTOP), 0, 2, dtype=jnp.int32)
    row_ids = jnp.arange(KTOP, dtype=jnp.int32)[:, None]
    col_ids = jnp.arange(KTOP, dtype=jnp.int32)[None, :]
    forced = jnp.logical_and(col_ids == 0, row_ids >= SPAN)
    return jnp.where(forced, jnp.ones_like(random_bits), random_bits)


def spiked(result, own_key, source, target, blocks, factor):
    def block_of(axis_at):
        return (jnp.arange(result.shape[axis_at]) // (result.shape[axis_at] // blocks)).reshape((-1,) + (1,) * (result.ndim - 1 - axis_at))

    near = jax.random.permutation(own_key, blocks)[block_of(target)]
    second = (block_of(target) + blocks // 2) % blocks
    return jnp.where((block_of(source) == near) | (block_of(source) == second), factor * result, result)


def level_of(own_key, extent, cuts, low, high):
    def one(dim, shards_of):
        draws = jax.random.uniform(jax.random.fold_in(jax.random.fold_in(own_key, 6), dim), (shards_of,), jnp.float32, low / len(cuts), high / len(cuts))
        return jnp.repeat(jnp.exp(draws), extent[dim] // shards_of).reshape((-1,) + (1,) * (len(extent) - dim - 1))

    loudness = one(*cuts[0])
    for cut in cuts[1:]:
        loudness = loudness * one(*cut)
    return loudness


def centred(rng, shape, width, most, shards=(), kind=jnp.bfloat16):
    result = width * jax.random.normal(rng, shape, jnp.float32)
    if shards:
        result = result * level_of(rng, shape, shards, -0.22, 0.18)
    return jnp.clip(result, -most, most).astype(kind)


def bell_draw_with(stream_key, shape, width, reach, pieces, heavy, kind=jnp.bfloat16):
    values = width * jax.random.normal(stream_key, shape, jnp.float32)
    if pieces:
        values = values * level_of(stream_key, shape, pieces, -0.22, 0.18)
    return jnp.clip(spiked(values, jax.random.fold_in(stream_key, 3), *heavy), -reach, reach).astype(kind)


def setup_inputs(seed: int = 0) -> dict:
    streams_of = jax.random.split(jax.random.key(seed), 15)
    leaf_inverse = draw_leaf_inverse(jax.random.fold_in(streams_of[14], 71), 0)
    leaf_coupling = centred(streams_of[1], (LAYERS, GROUP, LEAVES, BLOCK, BLOCK), BLOCK ** -0.5, 0.5, ((0, 4), (1, 32)), jnp.float32)
    leaf_rhs = centred(streams_of[2], (LAYERS, GROUP, LEAVES, BLOCK, NRHS), 1.0, 6.0, ((0, 4), (1, 32)), jnp.float32)
    mid_inverse = draw_mid_inverse(jax.random.fold_in(streams_of[14], 71), 0)
    mid_coupling = centred(streams_of[4], (LAYERS, GROUP, MIDS, BLOCK, BLOCK), (2 * BLOCK) ** -0.5, 0.375, ((0, 4), (1, 32)), jnp.float32)
    mid_rhs = centred(streams_of[5], (LAYERS, GROUP, MIDS, BLOCK, NRHS), 1.0, 6.0, ((0, 4), (1, 32)), jnp.float32)
    mid_top = bell_draw_with(streams_of[6], (LAYERS, GROUP, MIDS, KTOP * BLOCK, BLOCK), (3 * BLOCK * LAYERS * GROUP) ** -0.5, 0.0546875, ((0, 4), (1, 32)), (1, 3, 32, 2.75), jnp.float32)
    root_inverse = draw_root_inverse(jax.random.fold_in(streams_of[14], 71), 0)
    root_top = bell_draw_with(streams_of[8], (LAYERS, GROUP, KTOP * BLOCK, BLOCK), (3 * BLOCK * LAYERS * GROUP) ** -0.5, 0.0546875, ((0, 4), (1, 32)), (1, 2, 32, 2.75), jnp.float32)
    root_rhs = centred(streams_of[9], (LAYERS, GROUP, BLOCK, NRHS), 1.0, 6.0, ((0, 4), (1, 32)), jnp.float32)
    top_inverse = draw_top_inverse(jax.random.fold_in(streams_of[14], 71), 0)
    top_factor = centred(streams_of[11], (KTOP, BLOCK, KTOP * BLOCK), (KTOP * BLOCK // 9) ** -0.5, 0.25, ((0, 32),), jnp.float32)
    top_rhs = centred(streams_of[12], (KTOP, BLOCK, NRHS), 1.0, 6.0, ((0, 32),), jnp.float32)
    top_pattern = draw_top_pattern(jax.random.fold_in(streams_of[14], 71), 0)
    return dict(leaf_inverse=leaf_inverse, leaf_coupling=leaf_coupling, leaf_rhs=leaf_rhs, mid_inverse=mid_inverse, mid_coupling=mid_coupling, mid_rhs=mid_rhs, mid_top=mid_top, root_inverse=root_inverse, root_top=root_top, root_rhs=root_rhs, top_inverse=top_inverse, top_factor=top_factor, top_rhs=top_rhs, top_pattern=top_pattern)


def product(spec, left, right):
    return jnp.einsum(spec, left, right, precision=lax.Precision.HIGHEST, preferred_element_type=jnp.float32)


def reference(leaf_inverse, leaf_coupling, leaf_rhs, mid_inverse, mid_coupling, mid_rhs, mid_top, root_inverse, root_top, root_rhs, top_inverse, top_factor, top_rhs, top_pattern):
    forward_leaf = product('lgpab,lgpbr->lgpar', leaf_inverse, leaf_rhs)
    pulled = product('lgpab,lgpbr->lgpar', leaf_coupling, forward_leaf)
    pulled = pulled.reshape(LAYERS, GROUP, MIDS, 2, BLOCK, NRHS).sum(axis=3)
    forward_mid = product('lgmab,lgmbr->lgmar', mid_inverse, mid_rhs - pulled)
    root_input = root_rhs - product('lgmab,lgmbr->lgar', mid_coupling, forward_mid)
    forward_root = product('lgab,lgbr->lgar', root_inverse, root_input)
    gathered_terms = product('lgkb,lgbr->kr', root_top, forward_root) + product('lgmkb,lgmbr->kr', mid_top, forward_mid)
    residual_top = top_rhs - gathered_terms.reshape(KTOP, BLOCK, NRHS)
    blocks = top_factor.reshape(KTOP, BLOCK, KTOP, BLOCK)
    group_ids = jnp.arange(KTOP) // SPAN
    lower_part = group_ids[None, :] < group_ids[:, None]
    weights = jnp.where(lower_part, top_pattern, 0).astype(jnp.float32)
    forward_top = jnp.zeros((KTOP, BLOCK, NRHS), jnp.float32)
    for column in range(KTOP):
        solved = jnp.dot(top_inverse[column], residual_top[column], precision=lax.Precision.HIGHEST, preferred_element_type=jnp.float32)
        forward_top = forward_top.at[column].set(solved)
        update = product('kab,br->kar', blocks[:, :, column, :], solved)
        residual_top = residual_top - weights[:, column][:, None, None] * update
    back_top = jnp.zeros((KTOP, BLOCK, NRHS), jnp.float32)
    for sweep_step in range(KTOP):
        column = KTOP - 1 - sweep_step
        terms = product('kab,kar->kbr', blocks[:, :, column, :], back_top)
        pulled_top = jnp.sum(weights[:, column][:, None, None] * terms, axis=0)
        solved = jnp.dot(top_inverse[column].T, forward_top[column] - pulled_top, precision=lax.Precision.HIGHEST, preferred_element_type=jnp.float32)
        back_top = back_top.at[column].set(solved)
    flat_top = back_top.reshape(KTOP * BLOCK, NRHS)
    back_root = product('lgba,lgbr->lgar', root_inverse, forward_root - product('lgkb,kr->lgbr', root_top, flat_top))
    back_mid = product('lgmba,lgmbr->lgmar', mid_inverse, forward_mid - product('lgmab,lgar->lgmbr', mid_coupling, back_root) - product('lgmkb,kr->lgmbr', mid_top, flat_top))
    parent = jnp.repeat(back_mid, 2, axis=2)
    back_leaf = product('lgpba,lgpbr->lgpar', leaf_inverse, forward_leaf - product('lgpab,lgpar->lgpbr', leaf_coupling, parent))
    return back_leaf, back_mid, back_root, back_top
```

```python
import functools

import jax
import jax.numpy as jnp
from jax import lax
from jax.experimental import pallas as pl
from jax.experimental.pallas import tpu as pltpu
from jax.sharding import PartitionSpec as P

SPAN = 4
KTOP = 32
GROUPS = KTOP // SPAN
BLOCK = 128
KEEP = 14
SLOTS = KEEP + 1


def product(spec, left, right):
    return jnp.einsum(
        spec, left, right, precision=lax.Precision.HIGHEST, preferred_element_type=jnp.float32
    )


def sweep_kernel(rhs_ref, factor_hbm, out_ref, factor, forward, pulled, sems):
    copies = [
        pltpu.make_async_copy(
            factor_hbm.at[pl.ds(d * SLOTS, SLOTS)], factor.at[d], sems.at[d]
        )
        for d in range(KTOP)
    ]
    for copy in copies:
        copy.start()
    eye = lax.broadcasted_iota(jnp.int32, (BLOCK, BLOCK), 0) == lax.broadcasted_iota(
        jnp.int32, (BLOCK, BLOCK), 1
    )

    def fold(value):
        return jnp.broadcast_to(jnp.sum(value, axis=0, keepdims=True), (8, BLOCK))

    def tall(row):
        return jnp.concatenate([row] * (BLOCK // 8), axis=0)

    for i in range(KTOP):
        g = i // SPAN
        copies[i].wait()
        row = jnp.broadcast_to(rhs_ref[pl.ds(i, 1), :], (8, BLOCK))
        acc = jnp.where(eye, tall(row), 0.0)

        def add(j, acc, d, shift):
            return acc + factor[d, j - shift] * tall(forward[j])

        count = min(SPAN * g, KEEP)
        if count:
            acc = lax.fori_loop(
                0, count, functools.partial(add, d=i, shift=0), acc, unroll=2
            )
        if SPAN * g > KEEP:
            acc = lax.fori_loop(
                KEEP,
                SPAN * g,
                functools.partial(add, d=KTOP - 1 - i, shift=SPAN * g - KEEP),
                acc,
                unroll=2,
            )
        column = jnp.sum(acc, axis=1, keepdims=True)
        forward[i] = fold(factor[i, KEEP] * -column)

    pulled[...] = jnp.zeros_like(pulled)
    for i in range(KTOP - 1, -1, -1):
        g = i // SPAN
        row = forward[i] - jnp.broadcast_to(
            jnp.sum(pulled[i], axis=0, keepdims=True), (8, BLOCK)
        )
        column = jnp.sum(factor[i, KEEP] * tall(row), axis=1, keepdims=True)
        wide = jnp.broadcast_to(column, (BLOCK, BLOCK))
        out_ref[pl.ds(i, 1), :] = jnp.sum(jnp.where(eye, wide, 0.0), axis=0, keepdims=True)

        def pull(j, carry, d, shift):
            terms = factor[d, j - shift] * wide
            pulled[j] += jnp.sum(terms.reshape(BLOCK // 8, 8, BLOCK), axis=0)
            return carry

        count = min(SPAN * g, KEEP)
        if count:
            lax.fori_loop(0, count, functools.partial(pull, d=i, shift=0), 0, unroll=2)
        if SPAN * g > KEEP:
            lax.fori_loop(
                KEEP,
                SPAN * g,
                functools.partial(pull, d=KTOP - 1 - i, shift=SPAN * g - KEEP),
                0,
                unroll=2,
            )


def sweep(rhs, factor):
    return pl.pallas_call(
        sweep_kernel,
        out_shape=jax.ShapeDtypeStruct((KTOP, BLOCK), jnp.float32),
        in_specs=[pl.BlockSpec(memory_space=pltpu.VMEM), pl.BlockSpec(memory_space=pl.ANY)],
        out_specs=pl.BlockSpec(memory_space=pltpu.VMEM),
        scratch_shapes=[
            pltpu.VMEM((KTOP, SLOTS, BLOCK, BLOCK), jnp.float32),
            pltpu.VMEM((KTOP, 8, BLOCK), jnp.float32),
            pltpu.VMEM((KTOP, 8, BLOCK), jnp.float32),
            pltpu.SemaphoreType.DMA((KTOP,)),
        ],
        compiler_params=pltpu.CompilerParams(vmem_limit_bytes=44 * 2**20),
    )(rhs, factor)


def pack_rows(factor_row, pattern_row, inverse, position):
    own_group = position // SPAN
    column_groups = jnp.arange(KTOP) // SPAN
    weights = jnp.where(column_groups < own_group, pattern_row, 0).astype(jnp.float32)
    blocks = factor_row.reshape(BLOCK, KTOP, BLOCK).transpose(1, 0, 2) * weights[:, None, None]
    start = jnp.maximum(SPAN * own_group - KEEP, 0)
    excess = lax.dynamic_slice_in_dim(blocks, start, KEEP)
    got = lax.ppermute(excess, "grid", [(KTOP - 1 - d, d) for d in range(KTOP // 2)])
    own = (jnp.arange(KEEP) < SPAN * own_group)[:, None, None]
    packed = jnp.where(own, blocks[:KEEP], got)
    return jnp.concatenate([packed, inverse.T[None]], axis=0)


def local(
    leaf_inverse,
    leaf_coupling,
    leaf_rhs,
    mid_inverse,
    mid_coupling,
    mid_rhs,
    mid_top,
    root_inverse,
    root_top,
    root_rhs,
    top_inverse,
    top_factor,
    top_rhs,
    top_pattern,
):
    columns = leaf_rhs.shape[-1]
    position = lax.axis_index("grid")
    layer = lax.axis_index("layer")
    layers = lax.axis_size("layer")
    packed = pack_rows(top_factor[0], top_pattern[0], top_inverse[0], position)
    factor = lax.all_gather(packed, "grid", axis=0, tiled=True)

    leaf_inv = leaf_inverse[0, 0]
    leaf_links = leaf_coupling[0, 0]
    forward_leaf = product("pab,pbr->par", leaf_inv, leaf_rhs[0, 0])
    pulled = (
        product("pab,pbr->par", leaf_links, forward_leaf)
        .reshape(-1, 2, BLOCK, columns)
        .sum(axis=1)
    )
    forward_mid = product("mab,mbr->mar", mid_inverse[0, 0], mid_rhs[0, 0] - pulled)
    root_input = root_rhs[0, 0] - product("mab,mbr->ar", mid_coupling[0, 0], forward_mid)
    forward_root = product("ab,br->ar", root_inverse[0, 0], root_input)
    root_panel = root_top[0, 0]
    mid_panel = mid_top[0, 0]
    summed = product("br,kb->rk", forward_root, root_panel) + product(
        "mbr,mkb->rk", forward_mid, mid_panel
    )
    summed = summed.reshape(columns, KTOP, BLOCK)
    mine = ((jnp.arange(KTOP) == position) & (layer == 0))[None, :, None]
    summed = summed - jnp.where(mine, top_rhs[0].T[:, None, :], 0.0)
    summed = summed.reshape(KTOP, layers, KTOP, BLOCK).transpose(1, 0, 2, 3)
    summed = summed.reshape(columns, KTOP, BLOCK)
    parts = lax.all_to_all(summed, ("layer", "grid"), 0, 0, tiled=True)
    residual = parts.sum(axis=0)

    own_column = sweep(residual, factor)
    layer_columns = lax.all_gather(own_column, "layer", axis=0)
    grid = lax.axis_size("grid")
    everywhere = jnp.broadcast_to(layer_columns[None], (grid, layers, KTOP, BLOCK))
    solved = lax.all_to_all(everywhere, "grid", 0, 0, tiled=True)
    solved = solved.reshape(columns, KTOP, BLOCK)
    own_top = lax.dynamic_index_in_dim(solved, position, 1, keepdims=False).T
    flat = solved.reshape(columns, KTOP * BLOCK)
    root_pull = product("kb,rk->br", root_panel, flat)
    mid_pull = product("mkb,rk->mbr", mid_panel, flat)
    back_root = product("ba,br->ar", root_inverse[0, 0], forward_root - root_pull)
    back_mid = product(
        "mba,mbr->mar",
        mid_inverse[0, 0],
        forward_mid - product("mab,ar->mbr", mid_coupling[0, 0], back_root) - mid_pull,
    )
    parent = jnp.repeat(back_mid, 2, axis=0)
    back_leaf = product(
        "pba,pbr->par", leaf_inv, forward_leaf - product("pab,par->pbr", leaf_links, parent)
    )
    return (back_leaf[None, None], back_mid[None, None], back_root[None, None], own_top[None])


def solution(mesh):
    placed = (
        P("layer", "grid", None, None, None),
        P("layer", "grid", None, None, None),
        P("layer", "grid", None, None, None),
        P("layer", "grid", None, None, None),
        P("layer", "grid", None, None, None),
        P("layer", "grid", None, None, None),
        P("layer", "grid", None, None, None),
        P("layer", "grid", None, None),
        P("layer", "grid", None, None),
        P("layer", "grid", None, None),
        P("grid", None, None),
        P("grid", None, None),
        P("grid", None, None),
        P("grid", None),
    )
    return jax.shard_map(
        local,
        mesh=mesh,
        in_specs=placed,
        out_specs=(
            P("layer", "grid", None, None, None),
            P("layer", "grid", None, None, None),
            P("layer", "grid", None, None),
            P("grid", None, None),
        ),
        check_vma=False,
    )
```

```python
import functools

import jax
import jax.numpy as jnp
from jax import lax
from jax.experimental import pallas as pl
from jax.experimental.pallas import tpu as pltpu
from jax.sharding import Mesh, PartitionSpec as P

GRID = ("chip", "core")
SPAN = 4
KTOP = 32
GROUPS = KTOP // SPAN
BLOCK = 128
KEEP = 14
SLOTS = KEEP + 1


def product(spec, left, right):
    return jnp.einsum(
        spec, left, right, precision=lax.Precision.HIGHEST, preferred_element_type=jnp.float32
    )


def sweep_kernel(rhs_ref, factor_hbm, out_ref, factor, forward, pulled, sems):
    layers = factor_hbm.shape[0] // KTOP
    part = BLOCK // layers
    copies = [
        [
            pltpu.make_async_copy(
                factor_hbm.at[l * KTOP + d], factor.at[d, :, pl.ds(l * part, part)], sems.at[d, l]
            )
            for l in range(layers)
        ]
        for d in range(KTOP)
    ]
    for row_copies in copies:
        for copy in row_copies:
            copy.start()
    eye = lax.broadcasted_iota(jnp.int32, (BLOCK, BLOCK), 0) == lax.broadcasted_iota(
        jnp.int32, (BLOCK, BLOCK), 1
    )

    def fold(value):
        return jnp.broadcast_to(jnp.sum(value, axis=0, keepdims=True), (8, BLOCK))

    def tall(row):
        return jnp.concatenate([row] * (BLOCK // 8), axis=0)

    for i in range(KTOP):
        g = i // SPAN
        for copy in copies[i]:
            copy.wait()
        row = jnp.broadcast_to(rhs_ref[pl.ds(i, 1), :], (8, BLOCK))
        acc = jnp.where(eye, tall(row), 0.0)

        def add(j, acc, d, shift):
            return acc + factor[d, j - shift] * tall(forward[j])

        count = min(SPAN * g, KEEP)
        if count:
            acc = lax.fori_loop(
                0, count, functools.partial(add, d=i, shift=0), acc, unroll=2
            )
        if SPAN * g > KEEP:
            acc = lax.fori_loop(
                KEEP,
                SPAN * g,
                functools.partial(add, d=KTOP - 1 - i, shift=SPAN * g - KEEP),
                acc,
                unroll=2,
            )
        column = jnp.sum(acc, axis=1, keepdims=True)
        forward[i] = fold(factor[i, KEEP] * -column)

    pulled[...] = jnp.zeros_like(pulled)
    for i in range(KTOP - 1, -1, -1):
        g = i // SPAN
        row = forward[i] - jnp.broadcast_to(
            jnp.sum(pulled[i], axis=0, keepdims=True), (8, BLOCK)
        )
        column = jnp.sum(factor[i, KEEP] * tall(row), axis=1, keepdims=True)
        wide = jnp.broadcast_to(column, (BLOCK, BLOCK))
        out_ref[pl.ds(i, 1), :] = jnp.sum(jnp.where(eye, wide, 0.0), axis=0, keepdims=True)

        def pull(j, carry, d, shift):
            terms = factor[d, j - shift] * wide
            pulled[j] += jnp.sum(terms.reshape(BLOCK // 8, 8, BLOCK), axis=0)
            return carry

        count = min(SPAN * g, KEEP)
        if count:
            lax.fori_loop(0, count, functools.partial(pull, d=i, shift=0), 0, unroll=2)
        if SPAN * g > KEEP:
            lax.fori_loop(
                KEEP,
                SPAN * g,
                functools.partial(pull, d=KTOP - 1 - i, shift=SPAN * g - KEEP),
                0,
                unroll=2,
            )


def sweep(rhs, factor):
    return pl.pallas_call(
        sweep_kernel,
        out_shape=jax.ShapeDtypeStruct((KTOP, BLOCK), jnp.float32),
        in_specs=[pl.BlockSpec(memory_space=pltpu.VMEM), pl.BlockSpec(memory_space=pl.ANY)],
        out_specs=pl.BlockSpec(memory_space=pltpu.VMEM),
        scratch_shapes=[
            pltpu.VMEM((KTOP, SLOTS, BLOCK, BLOCK), jnp.float32),
            pltpu.VMEM((KTOP, 8, BLOCK), jnp.float32),
            pltpu.VMEM((KTOP, 8, BLOCK), jnp.float32),
            pltpu.SemaphoreType.DMA((KTOP, factor.shape[0] // KTOP)),
        ],
        compiler_params=pltpu.CompilerParams(vmem_limit_bytes=44 * 2**20),
    )(rhs, factor)


def pack_rows(factor_row, pattern_row, inverse, position, layer, layers):
    part = BLOCK // layers
    own_group = position // SPAN
    column_groups = jnp.arange(KTOP) // SPAN
    weights = jnp.where(column_groups < own_group, pattern_row, 0).astype(jnp.float32)
    rows = lax.dynamic_slice_in_dim(factor_row, layer * part, part)
    blocks = rows.reshape(part, KTOP, BLOCK).transpose(1, 0, 2) * weights[:, None, None]
    start = jnp.maximum(SPAN * own_group - KEEP, 0)
    excess = lax.dynamic_slice_in_dim(blocks, start, KEEP)
    got = lax.ppermute(excess, GRID, [(KTOP - 1 - d, d) for d in range(KTOP // 2)])
    own = (jnp.arange(KEEP) < SPAN * own_group)[:, None, None]
    packed = jnp.where(own, blocks[:KEEP], got)
    diagonal = lax.dynamic_slice_in_dim(inverse.T, layer * part, part)
    return jnp.concatenate([packed, diagonal[None]], axis=0)


def swap_cores(value):
    return lax.ppermute(value, "core", [(0, 1), (1, 0)])


def local(
    leaf_inverse,
    leaf_coupling,
    leaf_rhs,
    mid_inverse,
    mid_coupling,
    mid_rhs,
    mid_top,
    root_inverse,
    root_top,
    root_rhs,
    top_inverse,
    top_factor,
    top_rhs,
    top_pattern,
):
    columns = leaf_rhs.shape[-1]
    half = columns // 2
    position = lax.axis_index(GRID)
    core = lax.axis_index("core")
    layer = lax.axis_index("layer")
    layers = lax.axis_size("layer")
    packed = pack_rows(
        top_factor[0], top_pattern[0], top_inverse[0], position, layer, layers
    )
    factor = lax.all_gather(packed, ("layer",) + GRID, axis=0)

    leaf_inv = leaf_inverse[0, 0]
    leaf_links = leaf_coupling[0, 0]
    forward_leaf = product("pab,pbr->par", leaf_inv, leaf_rhs[0, 0])
    pulled = (
        product("pab,pbr->par", leaf_links, forward_leaf)
        .reshape(-1, 2, BLOCK, columns)
        .sum(axis=1)
    )
    forward_mid = product("mab,mbr->mar", mid_inverse[0, 0], mid_rhs[0, 0] - pulled)
    root_input = root_rhs[0, 0] - product("mab,mbr->ar", mid_coupling[0, 0], forward_mid)
    forward_root = product("ab,br->ar", root_inverse[0, 0], root_input)
    root_panel = root_top[0, 0]
    mid_panel = mid_top[0, 0]
    summed = product("br,kb->rk", forward_root, root_panel) + product(
        "mbr,mkb->rk", forward_mid, mid_panel
    )
    summed = summed.reshape(columns, KTOP, BLOCK)
    mine = ((jnp.arange(KTOP) == position) & (layer == 0))[None, :, None]
    summed = summed - jnp.where(mine, top_rhs[0].T[:, None, :], 0.0)
    away = lax.dynamic_slice_in_dim(summed, (1 - core) * half, half)
    home = lax.dynamic_slice_in_dim(summed, core * half, half)
    parts = lax.all_to_all(home + swap_cores(away), ("layer", "chip"), 0, 0, tiled=True)
    residual = parts.sum(axis=0)

    own_column = sweep(residual, factor)
    everywhere = jnp.broadcast_to(own_column[None], (half, KTOP, BLOCK))
    near = lax.all_to_all(everywhere, ("layer", "chip"), 0, 0, tiled=True)
    far = swap_cores(near)
    solved = jnp.concatenate(
        [jnp.where(core == 0, near, far), jnp.where(core == 0, far, near)], axis=0
    )
    own_top = lax.dynamic_index_in_dim(solved, position, 1, keepdims=False).T
    flat = solved.reshape(columns, KTOP * BLOCK)
    root_pull = product("kb,rk->br", root_panel, flat)
    mid_pull = product("mkb,rk->mbr", mid_panel, flat)
    back_root = product("ba,br->ar", root_inverse[0, 0], forward_root - root_pull)
    back_mid = product(
        "mba,mbr->mar",
        mid_inverse[0, 0],
        forward_mid - product("mab,ar->mbr", mid_coupling[0, 0], back_root) - mid_pull,
    )
    parent = jnp.repeat(back_mid, 2, axis=0)
    back_leaf = product(
        "pba,pbr->par", leaf_inv, forward_leaf - product("pab,par->pbr", leaf_links, parent)
    )
    return (back_leaf[None, None], back_mid[None, None], back_root[None, None], own_top[None])


def solution(mesh):
    layers, grid = mesh.devices.shape
    chips = Mesh(mesh.devices.reshape(layers, grid // 2, 2), ("layer",) + GRID)
    subtree = ("layer", GRID)
    placed = (
        P(*subtree, None, None, None),
        P(*subtree, None, None, None),
        P(*subtree, None, None, None),
        P(*subtree, None, None, None),
        P(*subtree, None, None, None),
        P(*subtree, None, None, None),
        P(*subtree, None, None, None),
        P(*subtree, None, None),
        P(*subtree, None, None),
        P(*subtree, None, None),
        P(GRID, None, None),
        P(GRID, None, None),
        P(GRID, None, None),
        P(GRID, None),
    )
    return jax.shard_map(
        local,
        mesh=chips,
        in_specs=placed,
        out_specs=(
            P(*subtree, None, None, None),
            P(*subtree, None, None, None),
            P(*subtree, None, None),
            P(GRID, None, None),
        ),
        check_vma=False,
    )
```

```python
import functools

import jax
import jax.numpy as jnp
from jax import lax
from jax.experimental import pallas as pl
from jax.experimental.pallas import tpu as pltpu
from jax.sharding import Mesh, PartitionSpec as P

GRID = ("chip", "core")
SPAN = 4
KTOP = 32
GROUPS = KTOP // SPAN
BLOCK = 128
KEEP = 14
SLOTS = KEEP + 1


def product(spec, left, right):
    return jnp.einsum(
        spec, left, right, precision=lax.Precision.HIGHEST, preferred_element_type=jnp.float32
    )


def sweep_kernel(rhs_ref, factor_hbm, out_ref, factor, forward, pulled, sums, sems):
    layers = factor_hbm.shape[0] // KTOP
    part = BLOCK // layers
    copies = [
        [
            pltpu.make_async_copy(
                factor_hbm.at[l * KTOP + d], factor.at[d, :, pl.ds(l * part, part)], sems.at[d, l]
            )
            for l in range(layers)
        ]
        for d in range(KTOP)
    ]
    for row_copies in copies:
        for copy in row_copies:
            copy.start()
    eye = lax.broadcasted_iota(jnp.int32, (BLOCK, BLOCK), 0) == lax.broadcasted_iota(
        jnp.int32, (BLOCK, BLOCK), 1
    )

    def fold(value):
        return jnp.broadcast_to(jnp.sum(value, axis=0, keepdims=True), (8, BLOCK))

    def tall(row):
        return jnp.concatenate([row] * (BLOCK // 8), axis=0)

    def add(j, acc, d, shift):
        return acc + factor[d, j - shift] * tall(forward[j])

    def pull(j, carry, d, shift, wide):
        terms = factor[d, j - shift] * wide
        pulled[j] += jnp.sum(terms.reshape(BLOCK // 8, 8, BLOCK), axis=0)
        return carry

    def over_row(i, step, carry, unroll):
        g = i // SPAN
        count = min(SPAN * g, KEEP)
        if count:
            body = functools.partial(step, d=i, shift=0)
            carry = lax.fori_loop(0, count, body, carry, unroll=unroll)
        if SPAN * g > KEEP:
            body = functools.partial(step, d=KTOP - 1 - i, shift=SPAN * g - KEEP)
            carry = lax.fori_loop(KEEP, SPAN * g, body, carry, unroll=unroll)
        return carry

    for g in range(GROUPS):
        rows = range(SPAN * g, SPAN * (g + 1))
        for i in rows:
            for copy in copies[i]:
                copy.wait()
            row = jnp.broadcast_to(rhs_ref[pl.ds(i, 1), :], (8, BLOCK))
            start = jnp.where(eye, tall(row), 0.0)
            sums[i % SPAN] = over_row(i, add, start, 2)
        residuals = [-jnp.sum(sums[i % SPAN], axis=1, keepdims=True) for i in rows]
        for i, column in zip(rows, residuals):
            forward[i] = fold(factor[i, KEEP] * column)

    pulled[...] = jnp.zeros_like(pulled)
    for g in range(GROUPS - 1, -1, -1):
        rows = range(SPAN * g, SPAN * (g + 1))
        inputs = [
            forward[i]
            - jnp.broadcast_to(jnp.sum(pulled[i], axis=0, keepdims=True), (8, BLOCK))
            for i in rows
        ]
        solved = [
            jnp.sum(factor[i, KEEP] * tall(row), axis=1, keepdims=True)
            for i, row in zip(rows, inputs)
        ]
        for i, column in zip(rows, solved):
            wide = jnp.broadcast_to(column, (BLOCK, BLOCK))
            sums[i % SPAN] = wide
            out_ref[pl.ds(i, 1), :] = jnp.sum(
                jnp.where(eye, wide, 0.0), axis=0, keepdims=True
            )
        for i in rows:
            if g:
                over_row(i, functools.partial(pull, wide=sums[i % SPAN]), 0, 2)


def sweep(rhs, factor):
    return pl.pallas_call(
        sweep_kernel,
        out_shape=jax.ShapeDtypeStruct((KTOP, BLOCK), jnp.float32),
        in_specs=[pl.BlockSpec(memory_space=pltpu.VMEM), pl.BlockSpec(memory_space=pl.ANY)],
        out_specs=pl.BlockSpec(memory_space=pltpu.VMEM),
        scratch_shapes=[
            pltpu.VMEM((KTOP, SLOTS, BLOCK, BLOCK), jnp.float32),
            pltpu.VMEM((KTOP, 8, BLOCK), jnp.float32),
            pltpu.VMEM((KTOP, 8, BLOCK), jnp.float32),
            pltpu.VMEM((SPAN, BLOCK, BLOCK), jnp.float32),
            pltpu.SemaphoreType.DMA((KTOP, factor.shape[0] // KTOP)),
        ],
        compiler_params=pltpu.CompilerParams(vmem_limit_bytes=44 * 2**20),
    )(rhs, factor)


def split(value):
    high = value.astype(jnp.bfloat16)
    return high, (value - high.astype(jnp.float32)).astype(jnp.bfloat16)


def dot3(left, right):
    (a, b), (c, d) = left, right
    dot = functools.partial(jnp.dot, preferred_element_type=jnp.float32)
    return dot(a, c) + (dot(a, d) + dot(b, c))


def finish_kernel(
    place_ref,
    near_ref,
    far_ref,
    root_panel_ref,
    mid_panel_ref,
    forward_root_ref,
    forward_mid_ref,
    forward_leaf_ref,
    root_inverse_ref,
    mid_inverse_ref,
    mid_coupling_ref,
    leaf_inverse_ref,
    leaf_coupling_ref,
    leaf_out,
    mid_out,
    root_out,
    top_out,
    acc,
):
    step = pl.program_id(0)
    half = near_ref.shape[0] // KTOP
    blocks = root_panel_ref.shape[0] // BLOCK
    mids = mid_panel_ref.shape[0]
    leaves = leaf_inverse_ref.shape[0]
    core = place_ref[1]

    def columns_of(block):
        return jnp.concatenate(
            [
                near_ref[pl.ds(block, half, stride=KTOP), :],
                far_ref[pl.ds(block, half, stride=KTOP), :],
            ],
            axis=0,
        )

    def ordered(value):
        return jnp.where(
            core == 0, value, jnp.concatenate([value[half:], value[:half]], axis=0)
        )

    @pl.when(step == 0)
    def _():
        acc[...] = jnp.zeros_like(acc)

    solved = split(
        jnp.concatenate([columns_of(step * blocks + t) for t in range(blocks)], axis=1)
    )
    acc[0] += dot3(solved, split(root_panel_ref[...]))
    for m in range(mids):
        acc[1 + m] += dot3(solved, split(mid_panel_ref[m]))

    @pl.when(step == pl.num_programs(0) - 1)
    def _():
        top_out[...] = ordered(columns_of(place_ref[0])).T
        pulls = [ordered(acc[n]).T for n in range(1 + mids)]
        root = dot3(split(root_inverse_ref[...]), split(forward_root_ref[...] - pulls[0]))
        root_out[...] = root
        root = split(root)
        for m in range(mids):
            term = dot3(split(mid_coupling_ref[m]), root)
            mid = dot3(
                split(mid_inverse_ref[m]), split(forward_mid_ref[m] - term - pulls[1 + m])
            )
            mid_out[m] = mid
            mid = split(mid)
            for p in range(m * leaves // mids, (m + 1) * leaves // mids):
                term = dot3(split(leaf_coupling_ref[p]), mid)
                leaf_out[p] = dot3(
                    split(leaf_inverse_ref[p]), split(forward_leaf_ref[p] - term)
                )


def finish(place, near, far, root_panel, mid_panel, *small):
    mids, leaves = mid_panel.shape[0], small[2].shape[0]
    steps = 8
    rows = KTOP * BLOCK // steps
    whole = pl.BlockSpec(memory_space=pltpu.VMEM)
    out = functools.partial(jax.ShapeDtypeStruct, dtype=jnp.float32)
    return pl.pallas_call(
        finish_kernel,
        grid=(steps,),
        out_shape=(
            out((leaves, BLOCK, BLOCK)),
            out((mids, BLOCK, BLOCK)),
            out((BLOCK, BLOCK)),
            out((BLOCK, BLOCK)),
        ),
        in_specs=[
            pl.BlockSpec(memory_space=pltpu.SMEM),
            whole,
            whole,
            pl.BlockSpec((rows, BLOCK), lambda t: (t, 0)),
            pl.BlockSpec((mids, rows, BLOCK), lambda t: (0, t, 0)),
        ]
        + [whole] * len(small),
        out_specs=(whole,) * 4,
        scratch_shapes=[pltpu.VMEM((1 + mids, BLOCK, BLOCK), jnp.float32)],
        compiler_params=pltpu.CompilerParams(vmem_limit_bytes=40 * 2**20),
    )(place, near, far, root_panel, mid_panel, *small)


def pack_rows(factor_row, pattern_row, inverse, position, layer, layers):
    part = BLOCK // layers
    own_group = position // SPAN
    column_groups = jnp.arange(KTOP) // SPAN
    weights = jnp.where(column_groups < own_group, pattern_row, 0).astype(jnp.float32)
    rows = lax.dynamic_slice_in_dim(factor_row, layer * part, part)
    blocks = rows.reshape(part, KTOP, BLOCK).transpose(1, 0, 2) * weights[:, None, None]
    start = jnp.maximum(SPAN * own_group - KEEP, 0)
    excess = lax.dynamic_slice_in_dim(blocks, start, KEEP)
    got = lax.ppermute(excess, GRID, [(KTOP - 1 - d, d) for d in range(KTOP // 2)])
    own = (jnp.arange(KEEP) < SPAN * own_group)[:, None, None]
    packed = jnp.where(own, blocks[:KEEP], got)
    diagonal = lax.dynamic_slice_in_dim(inverse.T, layer * part, part)
    return jnp.concatenate([packed, diagonal[None]], axis=0)


def swap_cores(value):
    return lax.ppermute(value, "core", [(0, 1), (1, 0)])


def local(
    leaf_inverse,
    leaf_coupling,
    leaf_rhs,
    mid_inverse,
    mid_coupling,
    mid_rhs,
    mid_top,
    root_inverse,
    root_top,
    root_rhs,
    top_inverse,
    top_factor,
    top_rhs,
    top_pattern,
):
    columns = leaf_rhs.shape[-1]
    half = columns // 2
    position = lax.axis_index(GRID)
    core = lax.axis_index("core")
    layer = lax.axis_index("layer")
    layers = lax.axis_size("layer")
    packed = pack_rows(
        top_factor[0], top_pattern[0], top_inverse[0], position, layer, layers
    )
    factor = lax.all_gather(packed, ("layer",) + GRID, axis=0)

    leaf_inv = leaf_inverse[0, 0]
    leaf_links = leaf_coupling[0, 0]
    forward_leaf = product("pab,pbr->par", leaf_inv, leaf_rhs[0, 0])
    pulled = (
        product("pab,pbr->par", leaf_links, forward_leaf)
        .reshape(-1, 2, BLOCK, columns)
        .sum(axis=1)
    )
    forward_mid = product("mab,mbr->mar", mid_inverse[0, 0], mid_rhs[0, 0] - pulled)
    root_input = root_rhs[0, 0] - product("mab,mbr->ar", mid_coupling[0, 0], forward_mid)
    forward_root = product("ab,br->ar", root_inverse[0, 0], root_input)
    root_panel = root_top[0, 0]
    mid_panel = mid_top[0, 0]
    summed = product("br,kb->rk", forward_root, root_panel) + product(
        "mbr,mkb->rk", forward_mid, mid_panel
    )
    summed = summed.reshape(columns, KTOP, BLOCK)
    mine = ((jnp.arange(KTOP) == position) & (layer == 0))[None, :, None]
    summed = summed - jnp.where(mine, top_rhs[0].T[:, None, :], 0.0)
    away = lax.dynamic_slice_in_dim(summed, (1 - core) * half, half)
    home = lax.dynamic_slice_in_dim(summed, core * half, half)
    parts = lax.all_to_all(home + swap_cores(away), ("layer", "chip"), 0, 0, tiled=True)
    residual = parts.sum(axis=0)

    own_column = sweep(residual, factor)
    everywhere = jnp.broadcast_to(own_column[None], (half, KTOP, BLOCK))
    near = lax.all_to_all(everywhere, ("layer", "chip"), 0, 0, tiled=True)
    far = swap_cores(near)
    back_leaf, back_mid, back_root, own_top = finish(
        jnp.stack([position, core]).astype(jnp.int32),
        near.reshape(half * KTOP, BLOCK),
        far.reshape(half * KTOP, BLOCK),
        root_panel,
        mid_panel,
        forward_root,
        forward_mid,
        forward_leaf,
        root_inverse[0, 0].T,
        mid_inverse[0, 0].transpose(0, 2, 1),
        mid_coupling[0, 0].transpose(0, 2, 1),
        leaf_inv.transpose(0, 2, 1),
        leaf_links.transpose(0, 2, 1),
    )
    return (back_leaf[None, None], back_mid[None, None], back_root[None, None], own_top[None])


def solution(mesh):
    layers, grid = mesh.devices.shape
    chips = Mesh(mesh.devices.reshape(layers, grid // 2, 2), ("layer",) + GRID)
    subtree = ("layer", GRID)
    placed = (
        P(*subtree, None, None, None),
        P(*subtree, None, None, None),
        P(*subtree, None, None, None),
        P(*subtree, None, None, None),
        P(*subtree, None, None, None),
        P(*subtree, None, None, None),
        P(*subtree, None, None, None),
        P(*subtree, None, None),
        P(*subtree, None, None),
        P(*subtree, None, None),
        P(GRID, None, None),
        P(GRID, None, None),
        P(GRID, None, None),
        P(GRID, None),
    )
    return jax.shard_map(
        local,
        mesh=chips,
        in_specs=placed,
        out_specs=(
            P(*subtree, None, None, None),
            P(*subtree, None, None, None),
            P(*subtree, None, None),
            P(GRID, None, None),
        ),
        check_vma=False,
    )
```

```python
import functools

import jax
import jax.numpy as jnp
from jax import lax
from jax.experimental import pallas as pl
from jax.experimental.pallas import tpu as pltpu
from jax.sharding import Mesh, PartitionSpec as P

GRID = ("chip", "core")
SPAN = 4
KTOP = 32
GROUPS = KTOP // SPAN
BLOCK = 128
KEEP = 14
SLOTS = KEEP + 1


def product(spec, left, right):
    return jnp.einsum(
        spec, left, right, precision=lax.Precision.HIGHEST, preferred_element_type=jnp.float32
    )


def sweep_kernel(rhs_ref, factor_hbm, out_ref, factor, forward, pulled, sums, sems):
    layers = factor_hbm.shape[0] // KTOP
    part = BLOCK // layers
    copies = [
        [
            pltpu.make_async_copy(
                factor_hbm.at[l * KTOP + d], factor.at[d, :, pl.ds(l * part, part)], sems.at[d, l]
            )
            for l in range(layers)
        ]
        for d in range(KTOP)
    ]
    for row_copies in copies:
        for copy in row_copies:
            copy.start()
    eye = lax.broadcasted_iota(jnp.int32, (BLOCK, BLOCK), 0) == lax.broadcasted_iota(
        jnp.int32, (BLOCK, BLOCK), 1
    )

    def fold(value):
        return jnp.broadcast_to(jnp.sum(value, axis=0, keepdims=True), (8, BLOCK))

    def tall(row):
        return jnp.concatenate([row] * (BLOCK // 8), axis=0)

    def add(j, acc, d, shift):
        return acc + factor[d, j - shift] * tall(forward[j])

    def pull(j, carry, d, shift, wide):
        terms = factor[d, j - shift] * wide
        pulled[j] += jnp.sum(terms.reshape(BLOCK // 8, 8, BLOCK), axis=0)
        return carry

    def over_row(i, step, carry, unroll):
        g = i // SPAN
        count = min(SPAN * g, KEEP)
        if count:
            body = functools.partial(step, d=i, shift=0)
            carry = lax.fori_loop(0, count, body, carry, unroll=unroll)
        if SPAN * g > KEEP:
            body = functools.partial(step, d=KTOP - 1 - i, shift=SPAN * g - KEEP)
            carry = lax.fori_loop(KEEP, SPAN * g, body, carry, unroll=unroll)
        return carry

    for g in range(GROUPS):
        rows = range(SPAN * g, SPAN * (g + 1))
        for i in rows:
            for copy in copies[i]:
                copy.wait()
            row = jnp.broadcast_to(rhs_ref[pl.ds(i, 1), :], (8, BLOCK))
            start = jnp.where(eye, tall(row), 0.0)
            sums[i % SPAN] = over_row(i, add, start, 2)
        residuals = [-jnp.sum(sums[i % SPAN], axis=1, keepdims=True) for i in rows]
        for i, column in zip(rows, residuals):
            forward[i] = fold(factor[i, KEEP] * column)

    pulled[...] = jnp.zeros_like(pulled)
    for g in range(GROUPS - 1, -1, -1):
        rows = range(SPAN * g, SPAN * (g + 1))
        inputs = [
            forward[i]
            - jnp.broadcast_to(jnp.sum(pulled[i], axis=0, keepdims=True), (8, BLOCK))
            for i in rows
        ]
        solved = [
            jnp.sum(factor[i, KEEP] * tall(row), axis=1, keepdims=True)
            for i, row in zip(rows, inputs)
        ]
        for i, column in zip(rows, solved):
            wide = jnp.broadcast_to(column, (BLOCK, BLOCK))
            sums[i % SPAN] = wide
            out_ref[pl.ds(i, 1), :] = jnp.sum(
                jnp.where(eye, wide, 0.0), axis=0, keepdims=True
            )
        for i in rows:
            if g:
                over_row(i, functools.partial(pull, wide=sums[i % SPAN]), 0, True)


def sweep(rhs, factor):
    return pl.pallas_call(
        sweep_kernel,
        out_shape=jax.ShapeDtypeStruct((KTOP, BLOCK), jnp.float32),
        in_specs=[pl.BlockSpec(memory_space=pltpu.VMEM), pl.BlockSpec(memory_space=pl.ANY)],
        out_specs=pl.BlockSpec(memory_space=pltpu.VMEM),
        scratch_shapes=[
            pltpu.VMEM((KTOP, SLOTS, BLOCK, BLOCK), jnp.float32),
            pltpu.VMEM((KTOP, 8, BLOCK), jnp.float32),
            pltpu.VMEM((KTOP, 8, BLOCK), jnp.float32),
            pltpu.VMEM((SPAN, BLOCK, BLOCK), jnp.float32),
            pltpu.SemaphoreType.DMA((KTOP, factor.shape[0] // KTOP)),
        ],
        compiler_params=pltpu.CompilerParams(vmem_limit_bytes=44 * 2**20),
    )(rhs, factor)


def split(value):
    high = value.astype(jnp.bfloat16)
    return high, (value - high.astype(jnp.float32)).astype(jnp.bfloat16)


def dot3(left, right):
    (a, b), (c, d) = left, right
    dot = functools.partial(jnp.dot, preferred_element_type=jnp.float32)
    return dot(a, c) + (dot(a, d) + dot(b, c))


def prepare_kernel(*refs):
    outs = refs[len(refs) // 2 :]
    for ref, out in zip(refs, outs):
        for n in range(ref.shape[0]):
            high, low = split(ref[n].T)
            out[n, 0] = high
            out[n, 1] = low


def prepare(*matrices):
    return pl.pallas_call(
        prepare_kernel,
        out_shape=tuple(
            jax.ShapeDtypeStruct((m.shape[0], 2) + m.shape[1:], jnp.bfloat16) for m in matrices
        ),
    )(*matrices)


def finish_kernel(
    place_ref,
    near_ref,
    far_ref,
    root_panel_ref,
    mid_panel_ref,
    forward_root_ref,
    forward_mid_ref,
    forward_leaf_ref,
    root_inverse_ref,
    mid_inverse_ref,
    mid_coupling_ref,
    leaf_inverse_ref,
    leaf_coupling_ref,
    leaf_out,
    mid_out,
    root_out,
    top_out,
    acc,
):
    step = pl.program_id(0)
    half = near_ref.shape[0] // KTOP
    blocks = root_panel_ref.shape[0] // BLOCK
    mids = mid_panel_ref.shape[0]
    leaves = leaf_inverse_ref.shape[0]
    core = place_ref[1]

    def columns_of(block):
        return jnp.concatenate(
            [
                near_ref[pl.ds(block, half, stride=KTOP), :],
                far_ref[pl.ds(block, half, stride=KTOP), :],
            ],
            axis=0,
        )

    def ordered(value):
        return jnp.where(
            core == 0, value, jnp.concatenate([value[half:], value[:half]], axis=0)
        )

    @pl.when(step == 0)
    def _():
        acc[...] = jnp.zeros_like(acc)

    solved = split(
        jnp.concatenate([columns_of(step * blocks + t) for t in range(blocks)], axis=1)
    )
    acc[0] += dot3(solved, split(root_panel_ref[...]))
    for m in range(mids):
        acc[1 + m] += dot3(solved, split(mid_panel_ref[m]))

    @pl.when(step == pl.num_programs(0) - 1)
    def _():
        top_out[...] = ordered(columns_of(place_ref[0])).T
        pulls = [ordered(acc[n]).T for n in range(1 + mids)]
        root = dot3((root_inverse_ref[0, 0], root_inverse_ref[0, 1]), split(forward_root_ref[...] - pulls[0]))
        root_out[...] = root
        root = split(root)
        for m in range(mids):
            term = dot3((mid_coupling_ref[m, 0], mid_coupling_ref[m, 1]), root)
            mid = dot3(
                (mid_inverse_ref[m, 0], mid_inverse_ref[m, 1]), split(forward_mid_ref[m] - term - pulls[1 + m])
            )
            mid_out[m] = mid
            mid = split(mid)
            for p in range(m * leaves // mids, (m + 1) * leaves // mids):
                term = dot3((leaf_coupling_ref[p, 0], leaf_coupling_ref[p, 1]), mid)
                leaf_out[p] = dot3(
                    (leaf_inverse_ref[p, 0], leaf_inverse_ref[p, 1]), split(forward_leaf_ref[p] - term)
                )


def finish(place, near, far, root_panel, mid_panel, *small):
    mids, leaves = mid_panel.shape[0], small[2].shape[0]
    steps = 8
    rows = KTOP * BLOCK // steps

    def whole(value):
        return pl.BlockSpec(value.shape, lambda t: (0,) * len(value.shape))

    out = functools.partial(jax.ShapeDtypeStruct, dtype=jnp.float32)
    shapes = (
        out((leaves, BLOCK, BLOCK)),
        out((mids, BLOCK, BLOCK)),
        out((BLOCK, BLOCK)),
        out((BLOCK, BLOCK)),
    )
    return pl.pallas_call(
        finish_kernel,
        grid=(steps,),
        out_shape=shapes,
        in_specs=[
            pl.BlockSpec(memory_space=pltpu.SMEM),
            whole(near),
            whole(far),
            pl.BlockSpec((rows, BLOCK), lambda t: (t, 0)),
            pl.BlockSpec((mids, rows, BLOCK), lambda t: (0, t, 0)),
        ]
        + [whole(value) for value in small],
        out_specs=tuple(whole(value) for value in shapes),
        scratch_shapes=[pltpu.VMEM((1 + mids, BLOCK, BLOCK), jnp.float32)],
        compiler_params=pltpu.CompilerParams(vmem_limit_bytes=60 * 2**20),
    )(place, near, far, root_panel, mid_panel, *small)


def pack_rows(factor_row, pattern_row, inverse, position, layer, layers):
    part = BLOCK // layers
    own_group = position // SPAN
    column_groups = jnp.arange(KTOP) // SPAN
    weights = jnp.where(column_groups < own_group, pattern_row, 0).astype(jnp.float32)
    rows = lax.dynamic_slice_in_dim(factor_row, layer * part, part)
    blocks = rows.reshape(part, KTOP, BLOCK).transpose(1, 0, 2) * weights[:, None, None]
    start = jnp.maximum(SPAN * own_group - KEEP, 0)
    excess = lax.dynamic_slice_in_dim(blocks, start, KEEP)
    got = lax.ppermute(excess, GRID, [(KTOP - 1 - d, d) for d in range(KTOP // 2)])
    own = (jnp.arange(KEEP) < SPAN * own_group)[:, None, None]
    packed = jnp.where(own, blocks[:KEEP], got)
    diagonal = lax.dynamic_slice_in_dim(inverse.T, layer * part, part)
    return jnp.concatenate([packed, diagonal[None]], axis=0)


def swap_cores(value):
    return lax.ppermute(value, "core", [(0, 1), (1, 0)])


def local(
    leaf_inverse,
    leaf_coupling,
    leaf_rhs,
    mid_inverse,
    mid_coupling,
    mid_rhs,
    mid_top,
    root_inverse,
    root_top,
    root_rhs,
    top_inverse,
    top_factor,
    top_rhs,
    top_pattern,
):
    columns = leaf_rhs.shape[-1]
    half = columns // 2
    position = lax.axis_index(GRID)
    core = lax.axis_index("core")
    layer = lax.axis_index("layer")
    layers = lax.axis_size("layer")
    packed = pack_rows(
        top_factor[0], top_pattern[0], top_inverse[0], position, layer, layers
    )
    factor = lax.all_gather(packed, ("layer",) + GRID, axis=0)

    leaf_inv = leaf_inverse[0, 0]
    leaf_links = leaf_coupling[0, 0]
    forward_leaf = product("pab,pbr->par", leaf_inv, leaf_rhs[0, 0])
    pulled = (
        product("pab,pbr->par", leaf_links, forward_leaf)
        .reshape(-1, 2, BLOCK, columns)
        .sum(axis=1)
    )
    forward_mid = product("mab,mbr->mar", mid_inverse[0, 0], mid_rhs[0, 0] - pulled)
    root_input = root_rhs[0, 0] - product("mab,mbr->ar", mid_coupling[0, 0], forward_mid)
    forward_root = product("ab,br->ar", root_inverse[0, 0], root_input)
    root_panel = root_top[0, 0]
    mid_panel = mid_top[0, 0]
    summed = product("br,kb->rk", forward_root, root_panel) + product(
        "mbr,mkb->rk", forward_mid, mid_panel
    )
    summed = summed.reshape(columns, KTOP, BLOCK)
    mine = ((jnp.arange(KTOP) == position) & (layer == 0))[None, :, None]
    summed = summed - jnp.where(mine, top_rhs[0].T[:, None, :], 0.0)
    prepared = prepare(
        root_inverse[0], mid_inverse[0, 0], mid_coupling[0, 0], leaf_inv, leaf_links
    )
    summed, prepared = lax.optimization_barrier((summed, prepared))
    away = lax.dynamic_slice_in_dim(summed, (1 - core) * half, half)
    home = lax.dynamic_slice_in_dim(summed, core * half, half)
    parts = lax.all_to_all(home + swap_cores(away), ("layer", "chip"), 0, 0, tiled=True)
    residual = parts.sum(axis=0)

    own_column = sweep(residual, factor)
    everywhere = jnp.broadcast_to(own_column[None], (half, KTOP, BLOCK))
    near = lax.all_to_all(everywhere, ("layer", "chip"), 0, 0, tiled=True)
    far = swap_cores(near)
    back_leaf, back_mid, back_root, own_top = finish(
        jnp.stack([position, core]).astype(jnp.int32),
        near.reshape(half * KTOP, BLOCK),
        far.reshape(half * KTOP, BLOCK),
        root_panel,
        mid_panel,
        forward_root,
        forward_mid,
        forward_leaf,
        *prepared,
    )
    return (back_leaf[None, None], back_mid[None, None], back_root[None, None], own_top[None])


def solution(mesh):
    layers, grid = mesh.devices.shape
    chips = Mesh(mesh.devices.reshape(layers, grid // 2, 2), ("layer",) + GRID)
    subtree = ("layer", GRID)
    placed = (
        P(*subtree, None, None, None),
        P(*subtree, None, None, None),
        P(*subtree, None, None, None),
        P(*subtree, None, None, None),
        P(*subtree, None, None, None),
        P(*subtree, None, None, None),
        P(*subtree, None, None, None),
        P(*subtree, None, None),
        P(*subtree, None, None),
        P(*subtree, None, None),
        P(GRID, None, None),
        P(GRID, None, None),
        P(GRID, None, None),
        P(GRID, None),
    )
    return jax.shard_map(
        local,
        mesh=chips,
        in_specs=placed,
        out_specs=(
            P(*subtree, None, None, None),
            P(*subtree, None, None, None),
            P(*subtree, None, None),
            P(GRID, None, None),
        ),
        check_vma=False,
    )
```

```python
import functools

import jax
import jax.numpy as jnp
from jax import lax
from jax.experimental import pallas as pl
from jax.experimental.pallas import tpu as pltpu
from jax.sharding import Mesh, PartitionSpec as P

GRID = ("chip", "core")
SPAN = 4
KTOP = 32
GROUPS = KTOP // SPAN
BLOCK = 128
KEEP = 14
SLOTS = KEEP + 1
MOVED = {
    4: ((14, 16, 8, 6),),
    5: ((14, 16, 8, 2), (16, 20, 12, 6)),
    6: ((14, 24, 24, 14),),
    7: ((14, 24, 24, 10), (24, 28, 28, 14)),
}
FIRST, SECOND = 10, 4


def product(spec, left, right):
    return jnp.einsum(
        spec, left, right, precision=lax.Precision.HIGHEST, preferred_element_type=jnp.float32
    )


def sweep_kernel(rhs_ref, factor_hbm, out_ref, factor, forward, pulled, sums, sems):
    layers = factor_hbm.shape[0] // KTOP
    copies = [
        [
            pltpu.make_async_copy(
                factor_hbm.at[l * KTOP + d], factor.at[l * KTOP + d], sems.at[d, l]
            )
            for l in range(layers)
        ]
        for d in range(KTOP)
    ]
    for row_copies in copies:
        for copy in row_copies:
            copy.start()
    eye = lax.broadcasted_iota(jnp.int32, (BLOCK, BLOCK), 0) == lax.broadcasted_iota(
        jnp.int32, (BLOCK, BLOCK), 1
    )

    def block(d, slot):
        return jnp.concatenate([factor[l * KTOP + d, slot] for l in range(layers)], axis=0)

    def fold(value):
        return jnp.broadcast_to(jnp.sum(value, axis=0, keepdims=True), (8, BLOCK))

    def tall(row):
        return jnp.concatenate([row] * (BLOCK // 8), axis=0)

    def add(j, acc, d, shift):
        return acc + block(d, j - shift) * tall(forward[j])

    def pull(j, carry, d, shift, wide):
        terms = block(d, j - shift) * wide
        pulled[j] += jnp.sum(terms.reshape(BLOCK // 8, 8, BLOCK), axis=0)
        return carry

    def over_row(i, step, carry, unroll):
        g = i // SPAN
        count = min(SPAN * g, KEEP)
        if count:
            body = functools.partial(step, d=i, shift=0)
            carry = lax.fori_loop(0, count, body, carry, unroll=unroll)
        for first, end, back, shift in MOVED.get(g, ()):
            body = functools.partial(step, d=i - back, shift=shift)
            carry = lax.fori_loop(first, end, body, carry, unroll=unroll)
        return carry

    for g in range(GROUPS):
        rows = range(SPAN * g, SPAN * (g + 1))
        for i in rows:
            for copy in copies[i]:
                copy.wait()
            row = jnp.broadcast_to(rhs_ref[pl.ds(i, 1), :], (8, BLOCK))
            start = jnp.where(eye, tall(row), 0.0)
            sums[i % SPAN] = over_row(i, add, start, 2)
        residuals = [-jnp.sum(sums[i % SPAN], axis=1, keepdims=True) for i in rows]
        for i, column in zip(rows, residuals):
            forward[i] = fold(block(i, KEEP) * column)

    pulled[...] = jnp.zeros_like(pulled)
    for g in range(GROUPS - 1, -1, -1):
        rows = range(SPAN * g, SPAN * (g + 1))
        inputs = [
            forward[i]
            - jnp.broadcast_to(jnp.sum(pulled[i], axis=0, keepdims=True), (8, BLOCK))
            for i in rows
        ]
        solved = [
            jnp.sum(block(i, KEEP) * tall(row), axis=1, keepdims=True)
            for i, row in zip(rows, inputs)
        ]
        for i, column in zip(rows, solved):
            wide = jnp.broadcast_to(column, (BLOCK, BLOCK))
            sums[i % SPAN] = wide
            out_ref[pl.ds(i, 1), :] = jnp.sum(
                jnp.where(eye, wide, 0.0), axis=0, keepdims=True
            )
        for i in rows:
            if g:
                over_row(i, functools.partial(pull, wide=sums[i % SPAN]), 0, True)


def sweep(rhs, factor):
    return pl.pallas_call(
        sweep_kernel,
        out_shape=jax.ShapeDtypeStruct((KTOP, BLOCK), jnp.float32),
        in_specs=[pl.BlockSpec(memory_space=pltpu.VMEM), pl.BlockSpec(memory_space=pl.ANY)],
        out_specs=pl.BlockSpec(memory_space=pltpu.VMEM),
        scratch_shapes=[
            pltpu.VMEM(factor.shape, jnp.float32),
            pltpu.VMEM((KTOP, 8, BLOCK), jnp.float32),
            pltpu.VMEM((KTOP, 8, BLOCK), jnp.float32),
            pltpu.VMEM((SPAN, BLOCK, BLOCK), jnp.float32),
            pltpu.SemaphoreType.DMA((KTOP, factor.shape[0] // KTOP)),
        ],
        compiler_params=pltpu.CompilerParams(vmem_limit_bytes=44 * 2**20),
    )(rhs, factor)


def split(value):
    high = value.astype(jnp.bfloat16)
    return high, (value - high.astype(jnp.float32)).astype(jnp.bfloat16)


def dot3(left, right):
    (a, b), (c, d) = left, right
    dot = functools.partial(jnp.dot, preferred_element_type=jnp.float32)
    return dot(a, c) + (dot(a, d) + dot(b, c))


def prepare_kernel(*refs):
    outs = refs[len(refs) // 2 :]
    for ref, out in zip(refs, outs):
        for n in range(ref.shape[0]):
            high, low = split(ref[n].T)
            out[n, 0] = high
            out[n, 1] = low


def prepare(*matrices):
    return pl.pallas_call(
        prepare_kernel,
        out_shape=tuple(
            jax.ShapeDtypeStruct((m.shape[0], 2) + m.shape[1:], jnp.bfloat16) for m in matrices
        ),
    )(*matrices)


def finish_kernel(
    place_ref,
    near_ref,
    far_ref,
    root_panel_ref,
    mid_panel_ref,
    forward_root_ref,
    forward_mid_ref,
    forward_leaf_ref,
    root_inverse_ref,
    mid_inverse_ref,
    mid_coupling_ref,
    leaf_inverse_ref,
    leaf_coupling_ref,
    leaf_out,
    mid_out,
    root_out,
    top_out,
    acc,
):
    step = pl.program_id(0)
    half = near_ref.shape[0] // KTOP
    blocks = root_panel_ref.shape[0] // BLOCK
    mids = mid_panel_ref.shape[0]
    leaves = leaf_inverse_ref.shape[0]
    core = place_ref[1]

    def columns_of(block):
        return jnp.concatenate(
            [
                near_ref[pl.ds(block, half, stride=KTOP), :],
                far_ref[pl.ds(block, half, stride=KTOP), :],
            ],
            axis=0,
        )

    def ordered(value):
        return jnp.where(
            core == 0, value, jnp.concatenate([value[half:], value[:half]], axis=0)
        )

    @pl.when(step == 0)
    def _():
        acc[...] = jnp.zeros_like(acc)

    solved = split(
        jnp.concatenate([columns_of(step * blocks + t) for t in range(blocks)], axis=1)
    )
    acc[0] += dot3(solved, split(root_panel_ref[...]))
    for m in range(mids):
        acc[1 + m] += dot3(solved, split(mid_panel_ref[m]))

    @pl.when(step == pl.num_programs(0) - 1)
    def _():
        top_out[...] = ordered(columns_of(place_ref[0])).T
        pulls = [ordered(acc[n]).T for n in range(1 + mids)]
        root = dot3((root_inverse_ref[0, 0], root_inverse_ref[0, 1]), split(forward_root_ref[...] - pulls[0]))
        root_out[...] = root
        root = split(root)
        for m in range(mids):
            term = dot3((mid_coupling_ref[m, 0], mid_coupling_ref[m, 1]), root)
            mid = dot3(
                (mid_inverse_ref[m, 0], mid_inverse_ref[m, 1]), split(forward_mid_ref[m] - term - pulls[1 + m])
            )
            mid_out[m] = mid
            mid = split(mid)
            for p in range(m * leaves // mids, (m + 1) * leaves // mids):
                term = dot3((leaf_coupling_ref[p, 0], leaf_coupling_ref[p, 1]), mid)
                leaf_out[p] = dot3(
                    (leaf_inverse_ref[p, 0], leaf_inverse_ref[p, 1]), split(forward_leaf_ref[p] - term)
                )


def finish(place, near, far, root_panel, mid_panel, *small):
    mids, leaves = mid_panel.shape[0], small[2].shape[0]
    steps = 8
    rows = KTOP * BLOCK // steps

    def whole(value):
        return pl.BlockSpec(value.shape, lambda t: (0,) * len(value.shape))

    out = functools.partial(jax.ShapeDtypeStruct, dtype=jnp.float32)
    shapes = (
        out((leaves, BLOCK, BLOCK)),
        out((mids, BLOCK, BLOCK)),
        out((BLOCK, BLOCK)),
        out((BLOCK, BLOCK)),
    )
    return pl.pallas_call(
        finish_kernel,
        grid=(steps,),
        out_shape=shapes,
        in_specs=[
            pl.BlockSpec(memory_space=pltpu.SMEM),
            whole(near),
            whole(far),
            pl.BlockSpec((rows, BLOCK), lambda t: (t, 0)),
            pl.BlockSpec((mids, rows, BLOCK), lambda t: (0, t, 0)),
        ]
        + [whole(value) for value in small],
        out_specs=tuple(whole(value) for value in shapes),
        scratch_shapes=[pltpu.VMEM((1 + mids, BLOCK, BLOCK), jnp.float32)],
        compiler_params=pltpu.CompilerParams(vmem_limit_bytes=60 * 2**20),
    )(place, near, far, root_panel, mid_panel, *small)


def pack_kernel(
    pattern_ref, inverse_ref, factor_hbm, keep_ref, first_ref, second_ref, rows, turned, sem
):
    part = rows.shape[0]
    layer = lax.axis_index("layer")
    own_group = (lax.axis_index("chip") * 2 + lax.axis_index("core")) // SPAN
    top = pl.multiple_of(layer * part, part)
    copy = pltpu.make_async_copy(factor_hbm.at[pl.ds(top, part)], rows, sem)
    copy.start()
    turned[...] = inverse_ref[...].T
    keep_ref[KEEP] = turned[pl.ds(top, part), :]
    copy.wait()

    def weighted(j):
        weight = jnp.where(j // SPAN < own_group, pattern_ref[0, j], 0).astype(jnp.float32)
        return rows[:, pl.ds(pl.multiple_of(j * BLOCK, BLOCK), BLOCK)] * weight

    for j in range(KEEP):
        keep_ref[j] = weighted(j)
    for t in range(FIRST):
        first_ref[t] = weighted(KEEP + t)
    start = jnp.where(own_group == 7, 24, 16)
    for t in range(SECOND):
        second_ref[t] = weighted(start + t)


def merge_kernel(keep_ref, first_ref, second_ref, out_ref):
    own_group = (lax.axis_index("chip") * 2 + lax.axis_index("core")) // SPAN
    own = SPAN * own_group
    out_ref[KEEP] = keep_ref[KEEP]
    for slot in range(KEEP):
        got = first_ref[jnp.clip(slot - own, 0, FIRST - 1)]
        if slot >= KEEP - SECOND:
            late = own_group % 2 == 0
            got = jnp.where(late, second_ref[slot - (KEEP - SECOND)], got)
        out_ref[slot] = jnp.where(slot < own, keep_ref[slot], got)


def pack_rows(factor_row, pattern_row, inverse, layers):
    part = BLOCK // layers
    out = functools.partial(jax.ShapeDtypeStruct, dtype=jnp.float32)
    vmem = pl.BlockSpec(memory_space=pltpu.VMEM)
    params = pltpu.CompilerParams(vmem_limit_bytes=60 * 2**20)
    keep, first, second = pl.pallas_call(
        pack_kernel,
        out_shape=(
            out((SLOTS, part, BLOCK)),
            out((FIRST, part, BLOCK)),
            out((SECOND, part, BLOCK)),
        ),
        in_specs=[
            pl.BlockSpec(memory_space=pltpu.SMEM),
            vmem,
            pl.BlockSpec(memory_space=pl.ANY),
        ],
        out_specs=(vmem,) * 3,
        scratch_shapes=[
            pltpu.VMEM((part, KTOP * BLOCK), jnp.float32),
            pltpu.VMEM((BLOCK, BLOCK), jnp.float32),
            pltpu.SemaphoreType.DMA,
        ],
        compiler_params=params,
    )(pattern_row, inverse, factor_row)
    moves = ([], [])
    for g, parts in MOVED.items():
        for move, (_, _, back, _) in zip(moves, parts):
            move += [(i, i - back) for i in range(SPAN * g, SPAN * (g + 1))]
    first = lax.ppermute(first, GRID, moves[0])
    second = lax.ppermute(second, GRID, moves[1])
    return pl.pallas_call(merge_kernel, out_shape=out((SLOTS, part, BLOCK)))(
        keep, first, second
    )


def swap_cores(value):
    return lax.ppermute(value, "core", [(0, 1), (1, 0)])


def local(
    leaf_inverse,
    leaf_coupling,
    leaf_rhs,
    mid_inverse,
    mid_coupling,
    mid_rhs,
    mid_top,
    root_inverse,
    root_top,
    root_rhs,
    top_inverse,
    top_factor,
    top_rhs,
    top_pattern,
):
    columns = leaf_rhs.shape[-1]
    half = columns // 2
    position = lax.axis_index(GRID)
    core = lax.axis_index("core")
    layer = lax.axis_index("layer")
    layers = lax.axis_size("layer")
    packed = pack_rows(top_factor[0], top_pattern, top_inverse[0], layers)
    factor = lax.all_gather(packed, ("layer",) + GRID, axis=0)

    leaf_inv = leaf_inverse[0, 0]
    leaf_links = leaf_coupling[0, 0]
    forward_leaf = product("pab,pbr->par", leaf_inv, leaf_rhs[0, 0])
    pulled = (
        product("pab,pbr->par", leaf_links, forward_leaf)
        .reshape(-1, 2, BLOCK, columns)
        .sum(axis=1)
    )
    forward_mid = product("mab,mbr->mar", mid_inverse[0, 0], mid_rhs[0, 0] - pulled)
    root_input = root_rhs[0, 0] - product("mab,mbr->ar", mid_coupling[0, 0], forward_mid)
    forward_root = product("ab,br->ar", root_inverse[0, 0], root_input)
    root_panel = root_top[0, 0]
    mid_panel = mid_top[0, 0]
    summed = product("br,kb->rk", forward_root, root_panel) + product(
        "mbr,mkb->rk", forward_mid, mid_panel
    )
    summed = summed.reshape(columns, KTOP, BLOCK)
    mine = ((jnp.arange(KTOP) == position) & (layer == 0))[None, :, None]
    summed = summed - jnp.where(mine, top_rhs[0].T[:, None, :], 0.0)
    prepared = prepare(
        root_inverse[0], mid_inverse[0, 0], mid_coupling[0, 0], leaf_inv, leaf_links
    )
    summed, prepared = lax.optimization_barrier((summed, prepared))
    away = lax.dynamic_slice_in_dim(summed, (1 - core) * half, half)
    home = lax.dynamic_slice_in_dim(summed, core * half, half)
    parts = lax.all_to_all(home + swap_cores(away), "layer", 0, 0, tiled=True)
    parts = parts.reshape(layers, half // layers, KTOP, BLOCK).sum(axis=0)
    residual = lax.all_to_all(parts, "chip", 0, 0, tiled=True).sum(axis=0)

    own_column = sweep(residual, factor)
    everywhere = jnp.broadcast_to(own_column[None], (half, KTOP, BLOCK))
    near = lax.all_to_all(everywhere, ("layer", "chip"), 0, 0, tiled=True)
    far = swap_cores(near)
    back_leaf, back_mid, back_root, own_top = finish(
        jnp.stack([position, core]).astype(jnp.int32),
        near.reshape(half * KTOP, BLOCK),
        far.reshape(half * KTOP, BLOCK),
        root_panel,
        mid_panel,
        forward_root,
        forward_mid,
        forward_leaf,
        *prepared,
    )
    return (back_leaf[None, None], back_mid[None, None], back_root[None, None], own_top[None])


def solution(mesh):
    layers, grid = mesh.devices.shape
    chips = Mesh(mesh.devices.reshape(layers, grid // 2, 2), ("layer",) + GRID)
    subtree = ("layer", GRID)
    placed = (
        P(*subtree, None, None, None),
        P(*subtree, None, None, None),
        P(*subtree, None, None, None),
        P(*subtree, None, None, None),
        P(*subtree, None, None, None),
        P(*subtree, None, None, None),
        P(*subtree, None, None, None),
        P(*subtree, None, None),
        P(*subtree, None, None),
        P(*subtree, None, None),
        P(GRID, None, None),
        P(GRID, None, None),
        P(GRID, None, None),
        P(GRID, None),
    )
    return jax.shard_map(
        local,
        mesh=chips,
        in_specs=placed,
        out_specs=(
            P(*subtree, None, None, None),
            P(*subtree, None, None, None),
            P(*subtree, None, None),
            P(GRID, None, None),
        ),
        check_vma=False,
    )
```

```python
import functools

import jax
import jax.numpy as jnp
from jax import lax
from jax.experimental import pallas as pl
from jax.experimental.pallas import tpu as pltpu
from jax.sharding import Mesh, PartitionSpec as P

GRID = ("chip", "core")
SPAN = 4
KTOP = 32
GROUPS = KTOP // SPAN
BLOCK = 128
NRHS = 128
KEEP = 14
SLOTS = KEEP + 1
MOVED = {
    4: ((14, 16, lambda i: i - 8, 6),),
    5: ((14, 16, lambda i: i - 8, 2), (16, 20, lambda i: (i - 12) ^ 2, 6)),
    6: ((14, 24, lambda i: i - 24, 14),),
    7: ((14, 24, lambda i: i - 24, 10), (24, 28, lambda i: (i - 28) ^ 2, 14)),
}
FIRST, SECOND = 10, 4


def product(spec, left, right):
    return jnp.einsum(
        spec, left, right, precision=lax.Precision.HIGHEST, preferred_element_type=jnp.float32
    )


def sweep_kernel(rhs_ref, factor_hbm, out_ref, factor, forward, pulled, sums, sems):
    layers = factor_hbm.shape[0] // KTOP
    copies = [
        [
            pltpu.make_async_copy(
                factor_hbm.at[l * KTOP + d], factor.at[l * KTOP + d], sems.at[d, l]
            )
            for l in range(layers)
        ]
        for d in range(KTOP)
    ]
    for row_copies in copies:
        for copy in row_copies:
            copy.start()
    eye = lax.broadcasted_iota(jnp.int32, (BLOCK, BLOCK), 0) == lax.broadcasted_iota(
        jnp.int32, (BLOCK, BLOCK), 1
    )

    def block(d, slot):
        return jnp.concatenate([factor[l * KTOP + d, slot] for l in range(layers)], axis=0)

    def fold(value):
        return jnp.broadcast_to(jnp.sum(value, axis=0, keepdims=True), (8, BLOCK))

    def tall(row):
        return jnp.concatenate([row] * (BLOCK // 8), axis=0)

    def add(j, acc, d, shift):
        return acc + block(d, j - shift) * tall(forward[j])

    def pull(j, carry, d, shift, wide):
        terms = block(d, j - shift) * wide
        pulled[j] += jnp.sum(terms.reshape(BLOCK // 8, 8, BLOCK), axis=0)
        return carry

    def over_row(i, step, carry, unroll):
        g = i // SPAN
        count = min(SPAN * g, KEEP)
        if count:
            body = functools.partial(step, d=i, shift=0)
            carry = lax.fori_loop(0, count, body, carry, unroll=unroll)
        for first, end, device, shift in MOVED.get(g, ()):
            body = functools.partial(step, d=device(i), shift=shift)
            carry = lax.fori_loop(first, end, body, carry, unroll=unroll)
        return carry

    for g in range(GROUPS):
        rows = range(SPAN * g, SPAN * (g + 1))
        for i in rows:
            for copy in copies[i]:
                copy.wait()
            row = jnp.broadcast_to(rhs_ref[pl.ds(i, 1), :], (8, BLOCK))
            start = jnp.where(eye, tall(row), 0.0)
            sums[i % SPAN] = over_row(i, add, start, 2)
        residuals = [-jnp.sum(sums[i % SPAN], axis=1, keepdims=True) for i in rows]
        for i, column in zip(rows, residuals):
            forward[i] = fold(block(i, KEEP) * column)

    pulled[...] = jnp.zeros_like(pulled)
    for g in range(GROUPS - 1, -1, -1):
        rows = range(SPAN * g, SPAN * (g + 1))
        inputs = [
            forward[i]
            - jnp.broadcast_to(jnp.sum(pulled[i], axis=0, keepdims=True), (8, BLOCK))
            for i in rows
        ]
        solved = [
            jnp.sum(block(i, KEEP) * tall(row), axis=1, keepdims=True)
            for i, row in zip(rows, inputs)
        ]
        for i, column in zip(rows, solved):
            wide = jnp.broadcast_to(column, (BLOCK, BLOCK))
            sums[i % SPAN] = wide
            out_ref[pl.ds(i, 1), :] = jnp.sum(
                jnp.where(eye, wide, 0.0), axis=0, keepdims=True
            )
        for i in rows:
            if g:
                over_row(i, functools.partial(pull, wide=sums[i % SPAN]), 0, True)


def sweep(rhs, factor):
    return pl.pallas_call(
        sweep_kernel,
        out_shape=jax.ShapeDtypeStruct((KTOP, BLOCK), jnp.float32),
        in_specs=[pl.BlockSpec(memory_space=pltpu.VMEM), pl.BlockSpec(memory_space=pl.ANY)],
        out_specs=pl.BlockSpec(memory_space=pltpu.VMEM),
        scratch_shapes=[
            pltpu.VMEM(factor.shape, jnp.float32),
            pltpu.VMEM((KTOP, 8, BLOCK), jnp.float32),
            pltpu.VMEM((KTOP, 8, BLOCK), jnp.float32),
            pltpu.VMEM((SPAN, BLOCK, BLOCK), jnp.float32),
            pltpu.SemaphoreType.DMA((KTOP, factor.shape[0] // KTOP)),
        ],
        compiler_params=pltpu.CompilerParams(vmem_limit_bytes=44 * 2**20),
    )(rhs, factor)


def split(value):
    high = value.astype(jnp.bfloat16)
    return high, (value - high.astype(jnp.float32)).astype(jnp.bfloat16)


def dot3(left, right):
    (a, b), (c, d) = left, right
    dot = functools.partial(jnp.dot, preferred_element_type=jnp.float32)
    both = dot(jnp.concatenate([a, b], axis=0), c)
    rows = a.shape[0]
    return both[:rows] + (dot(a, d) + both[rows:])


def prepare_kernel(*refs):
    outs = refs[len(refs) // 2 :]
    for ref, out in zip(refs, outs):
        for n in range(ref.shape[0]):
            high, low = split(ref[n].T)
            out[n, 0] = high
            out[n, 1] = low


def prepare(*matrices):
    return pl.pallas_call(
        prepare_kernel,
        out_shape=tuple(
            jax.ShapeDtypeStruct((m.shape[0], 2) + m.shape[1:], jnp.bfloat16) for m in matrices
        ),
    )(*matrices)


def finish_kernel(
    place_ref,
    near_ref,
    far_ref,
    root_panel_ref,
    mid_panel_ref,
    forward_root_ref,
    forward_mid_ref,
    forward_leaf_ref,
    root_inverse_ref,
    mid_inverse_ref,
    mid_coupling_ref,
    leaf_inverse_ref,
    leaf_coupling_ref,
    leaf_out,
    mid_out,
    root_out,
    top_out,
    acc,
):
    step = pl.program_id(0)
    half = near_ref.shape[0] // KTOP
    blocks = root_panel_ref.shape[0] // BLOCK
    mids = mid_panel_ref.shape[0]
    leaves = leaf_inverse_ref.shape[0]
    core = place_ref[1]

    def columns_of(block):
        return jnp.concatenate(
            [
                near_ref[pl.ds(block, half, stride=KTOP), :],
                far_ref[pl.ds(block, half, stride=KTOP), :],
            ],
            axis=0,
        )

    def ordered(value):
        return jnp.where(
            core == 0, value, jnp.concatenate([value[half:], value[:half]], axis=0)
        )

    @pl.when(step == 0)
    def _():
        acc[...] = jnp.zeros_like(acc)

    solved = split(
        jnp.concatenate([columns_of(step * blocks + t) for t in range(blocks)], axis=1)
    )
    panels = [root_panel_ref[...]] + [mid_panel_ref[m] for m in range(mids)]
    acc[...] += dot3(solved, split(jnp.concatenate(panels, axis=1)))

    @pl.when(step == pl.num_programs(0) - 1)
    def _():
        top_out[...] = ordered(columns_of(place_ref[0])).T
        pulls = [ordered(acc[:, n * BLOCK : (n + 1) * BLOCK]).T for n in range(1 + mids)]
        root = dot3((root_inverse_ref[0, 0], root_inverse_ref[0, 1]), split(forward_root_ref[...] - pulls[0]))
        root_out[...] = root
        root = split(root)
        for m in range(mids):
            term = dot3((mid_coupling_ref[m, 0], mid_coupling_ref[m, 1]), root)
            mid = dot3(
                (mid_inverse_ref[m, 0], mid_inverse_ref[m, 1]), split(forward_mid_ref[m] - term - pulls[1 + m])
            )
            mid_out[m] = mid
            mid = split(mid)
            for p in range(m * leaves // mids, (m + 1) * leaves // mids):
                term = dot3((leaf_coupling_ref[p, 0], leaf_coupling_ref[p, 1]), mid)
                leaf_out[p] = dot3(
                    (leaf_inverse_ref[p, 0], leaf_inverse_ref[p, 1]), split(forward_leaf_ref[p] - term)
                )


def finish(place, near, far, root_panel, mid_panel, *small):
    mids, leaves = mid_panel.shape[0], small[2].shape[0]
    steps = 4
    rows = KTOP * BLOCK // steps

    def whole(value):
        return pl.BlockSpec(value.shape, lambda t: (0,) * len(value.shape))

    out = functools.partial(jax.ShapeDtypeStruct, dtype=jnp.float32)
    shapes = (
        out((leaves, BLOCK, BLOCK)),
        out((mids, BLOCK, BLOCK)),
        out((BLOCK, BLOCK)),
        out((BLOCK, BLOCK)),
    )
    return pl.pallas_call(
        finish_kernel,
        grid=(steps,),
        out_shape=shapes,
        in_specs=[
            pl.BlockSpec(memory_space=pltpu.SMEM),
            whole(near),
            whole(far),
            pl.BlockSpec((rows, BLOCK), lambda t: (t, 0)),
            pl.BlockSpec((mids, rows, BLOCK), lambda t: (0, t, 0)),
        ]
        + [whole(value) for value in small],
        out_specs=tuple(whole(value) for value in shapes),
        scratch_shapes=[pltpu.VMEM((NRHS, (1 + mids) * BLOCK), jnp.float32)],
        compiler_params=pltpu.CompilerParams(vmem_limit_bytes=60 * 2**20),
    )(place, near, far, root_panel, mid_panel, *small)


def pack_kernel(
    pattern_ref, inverse_ref, factor_hbm, keep_ref, first_ref, second_ref, rows, turned, sem
):
    part = rows.shape[0]
    layer = lax.axis_index("layer")
    own_group = (lax.axis_index("chip") * 2 + lax.axis_index("core")) // SPAN
    top = pl.multiple_of(layer * part, part)
    copy = pltpu.make_async_copy(factor_hbm.at[pl.ds(top, part)], rows, sem)
    copy.start()
    turned[...] = inverse_ref[...].T
    keep_ref[KEEP] = turned[pl.ds(top, part), :]
    copy.wait()

    def weighted(j):
        weight = jnp.where(j // SPAN < own_group, pattern_ref[0, j], 0).astype(jnp.float32)
        return rows[:, pl.ds(pl.multiple_of(j * BLOCK, BLOCK), BLOCK)] * weight

    for j in range(KEEP):
        keep_ref[j] = weighted(j)
    for t in range(FIRST):
        first_ref[t] = weighted(KEEP + t)
    start = jnp.where(own_group == 7, 24, 16)
    for t in range(SECOND):
        second_ref[t] = weighted(start + t)


def merge_kernel(keep_ref, first_ref, second_ref, out_ref):
    own_group = (lax.axis_index("chip") * 2 + lax.axis_index("core")) // SPAN
    own = SPAN * own_group
    out_ref[KEEP] = keep_ref[KEEP]
    for slot in range(KEEP):
        got = first_ref[jnp.clip(slot - own, 0, FIRST - 1)]
        if slot >= KEEP - SECOND:
            late = own_group % 2 == 0
            got = jnp.where(late, second_ref[slot - (KEEP - SECOND)], got)
        out_ref[slot] = jnp.where(slot < own, keep_ref[slot], got)


def pack_rows(factor_row, pattern_row, inverse, layers):
    part = BLOCK // layers
    out = functools.partial(jax.ShapeDtypeStruct, dtype=jnp.float32)
    vmem = pl.BlockSpec(memory_space=pltpu.VMEM)
    params = pltpu.CompilerParams(vmem_limit_bytes=60 * 2**20)
    keep, first, second = pl.pallas_call(
        pack_kernel,
        out_shape=(
            out((SLOTS, part, BLOCK)),
            out((FIRST, part, BLOCK)),
            out((SECOND, part, BLOCK)),
        ),
        in_specs=[
            pl.BlockSpec(memory_space=pltpu.SMEM),
            vmem,
            pl.BlockSpec(memory_space=pl.ANY),
        ],
        out_specs=(vmem,) * 3,
        scratch_shapes=[
            pltpu.VMEM((part, KTOP * BLOCK), jnp.float32),
            pltpu.VMEM((BLOCK, BLOCK), jnp.float32),
            pltpu.SemaphoreType.DMA,
        ],
        compiler_params=params,
    )(pattern_row, inverse, factor_row)
    moves = ([], [])
    for g, parts in MOVED.items():
        for move, (_, _, device, _) in zip(moves, parts):
            move += [(i, device(i)) for i in range(SPAN * g, SPAN * (g + 1))]
    first = lax.ppermute(first, GRID, moves[0])
    second = lax.ppermute(second, GRID, moves[1])
    return pl.pallas_call(merge_kernel, out_shape=out((SLOTS, part, BLOCK)))(
        keep, first, second
    )


def swap_cores(value):
    return lax.ppermute(value, "core", [(0, 1), (1, 0)])


def local(
    leaf_inverse,
    leaf_coupling,
    leaf_rhs,
    mid_inverse,
    mid_coupling,
    mid_rhs,
    mid_top,
    root_inverse,
    root_top,
    root_rhs,
    top_inverse,
    top_factor,
    top_rhs,
    top_pattern,
):
    columns = leaf_rhs.shape[-1]
    half = columns // 2
    position = lax.axis_index(GRID)
    core = lax.axis_index("core")
    layer = lax.axis_index("layer")
    layers = lax.axis_size("layer")
    packed = pack_rows(top_factor[0], top_pattern, top_inverse[0], layers)
    factor = lax.all_gather(packed, ("layer",) + GRID, axis=0)

    leaf_inv = leaf_inverse[0, 0]
    leaf_links = leaf_coupling[0, 0]
    forward_leaf = product("pab,pbr->par", leaf_inv, leaf_rhs[0, 0])
    pulled = (
        product("pab,pbr->par", leaf_links, forward_leaf)
        .reshape(-1, 2, BLOCK, columns)
        .sum(axis=1)
    )
    forward_mid = product("mab,mbr->mar", mid_inverse[0, 0], mid_rhs[0, 0] - pulled)
    root_input = root_rhs[0, 0] - product("mab,mbr->ar", mid_coupling[0, 0], forward_mid)
    forward_root = product("ab,br->ar", root_inverse[0, 0], root_input)
    root_panel = root_top[0, 0]
    mid_panel = mid_top[0, 0]
    summed = product("br,kb->rk", forward_root, root_panel) + product(
        "mbr,mkb->rk", forward_mid, mid_panel
    )
    summed = summed.reshape(columns, KTOP, BLOCK)
    mine = ((jnp.arange(KTOP) == position) & (layer == 0))[None, :, None]
    summed = summed - jnp.where(mine, top_rhs[0].T[:, None, :], 0.0)
    prepared = prepare(
        root_inverse[0], mid_inverse[0, 0], mid_coupling[0, 0], leaf_inv, leaf_links
    )
    summed, prepared = lax.optimization_barrier((summed, prepared))
    away = lax.dynamic_slice_in_dim(summed, (1 - core) * half, half)
    home = lax.dynamic_slice_in_dim(summed, core * half, half)
    parts = lax.all_to_all(home + swap_cores(away), "layer", 0, 0, tiled=True)
    parts = parts.reshape(layers, half // layers, KTOP, BLOCK).sum(axis=0)
    residual = lax.all_to_all(parts, "chip", 0, 0, tiled=True).sum(axis=0)

    own_column = sweep(residual, factor)
    everywhere = jnp.broadcast_to(own_column[None], (half, KTOP, BLOCK))
    near = lax.all_to_all(everywhere, ("layer", "chip"), 0, 0, tiled=True)
    far = swap_cores(near)
    back_leaf, back_mid, back_root, own_top = finish(
        jnp.stack([position, core]).astype(jnp.int32),
        near.reshape(half * KTOP, BLOCK),
        far.reshape(half * KTOP, BLOCK),
        root_panel,
        mid_panel,
        forward_root,
        forward_mid,
        forward_leaf,
        *prepared,
    )
    return (back_leaf[None, None], back_mid[None, None], back_root[None, None], own_top[None])


def solution(mesh):
    layers, grid = mesh.devices.shape
    chips = Mesh(mesh.devices.reshape(layers, grid // 2, 2), ("layer",) + GRID)
    subtree = ("layer", GRID)
    placed = (
        P(*subtree, None, None, None),
        P(*subtree, None, None, None),
        P(*subtree, None, None, None),
        P(*subtree, None, None, None),
        P(*subtree, None, None, None),
        P(*subtree, None, None, None),
        P(*subtree, None, None, None),
        P(*subtree, None, None),
        P(*subtree, None, None),
        P(*subtree, None, None),
        P(GRID, None, None),
        P(GRID, None, None),
        P(GRID, None, None),
        P(GRID, None),
    )
    return jax.shard_map(
        local,
        mesh=chips,
        in_specs=placed,
        out_specs=(
            P(*subtree, None, None, None),
            P(*subtree, None, None, None),
            P(*subtree, None, None),
            P(GRID, None, None),
        ),
        check_vma=False,
    )
```

```python
import functools

import jax
import jax.numpy as jnp
from jax import lax
from jax.experimental import pallas as pl
from jax.experimental.pallas import tpu as pltpu
from jax.sharding import Mesh, PartitionSpec as P

GRID = ("chip", "core")
SPAN = 4
KTOP = 32
GROUPS = KTOP // SPAN
BLOCK = 128
NRHS = 128
KEEP = 14
SLOTS = KEEP + 1
MOVED = {
    4: ((14, 16, lambda i: i - 8, 6),),
    5: ((14, 16, lambda i: i - 8, 2), (16, 20, lambda i: (i - 12) ^ 2, 6)),
    6: ((14, 24, lambda i: i - 24, 14),),
    7: ((14, 24, lambda i: i - 24, 10), (24, 28, lambda i: (i - 28) ^ 2, 14)),
}
FIRST, SECOND = 10, 4


def product(spec, left, right):
    return jnp.einsum(
        spec, left, right, precision=lax.Precision.HIGHEST, preferred_element_type=jnp.float32
    )


def sweep_kernel(rhs_ref, factor_hbm, out_ref, factor, forward, pulled, sums, sems):
    layers = factor_hbm.shape[0] // KTOP
    copies = [
        [
            pltpu.make_async_copy(
                factor_hbm.at[l * KTOP + d], factor.at[l * KTOP + d], sems.at[d, l]
            )
            for l in range(layers)
        ]
        for d in range(KTOP)
    ]
    for row_copies in copies:
        for copy in row_copies:
            copy.start()
    eye = lax.broadcasted_iota(jnp.int32, (BLOCK, BLOCK), 0) == lax.broadcasted_iota(
        jnp.int32, (BLOCK, BLOCK), 1
    )

    def block(d, slot):
        return jnp.concatenate([factor[l * KTOP + d, slot] for l in range(layers)], axis=0)

    def fold(value):
        return jnp.broadcast_to(jnp.sum(value, axis=0, keepdims=True), (8, BLOCK))

    def tall(row):
        return jnp.concatenate([row] * (BLOCK // 8), axis=0)

    def add(j, acc, d, shift):
        return acc + block(d, j - shift) * tall(forward[j])

    def pull(j, carry, d, shift, wide):
        terms = block(d, j - shift) * wide
        pulled[j] += jnp.sum(terms.reshape(BLOCK // 8, 8, BLOCK), axis=0)
        return carry

    def over_row(i, step, carry, unroll):
        g = i // SPAN
        count = min(SPAN * g, KEEP)
        if count:
            body = functools.partial(step, d=i, shift=0)
            carry = lax.fori_loop(0, count, body, carry, unroll=unroll)
        for first, end, device, shift in MOVED.get(g, ()):
            body = functools.partial(step, d=device(i), shift=shift)
            carry = lax.fori_loop(first, end, body, carry, unroll=unroll)
        return carry

    for g in range(GROUPS):
        rows = range(SPAN * g, SPAN * (g + 1))
        for i in rows:
            for copy in copies[i]:
                copy.wait()
            row = jnp.broadcast_to(rhs_ref[pl.ds(i, 1), :], (8, BLOCK))
            start = jnp.where(eye, tall(row), 0.0)
            sums[i % SPAN] = over_row(i, add, start, 2)
        residuals = [-jnp.sum(sums[i % SPAN], axis=1, keepdims=True) for i in rows]
        for i, column in zip(rows, residuals):
            forward[i] = fold(block(i, KEEP) * column)

    pulled[...] = jnp.zeros_like(pulled)
    for g in range(GROUPS - 1, -1, -1):
        rows = range(SPAN * g, SPAN * (g + 1))
        inputs = [
            forward[i]
            - jnp.broadcast_to(jnp.sum(pulled[i], axis=0, keepdims=True), (8, BLOCK))
            for i in rows
        ]
        solved = [
            jnp.sum(block(i, KEEP) * tall(row), axis=1, keepdims=True)
            for i, row in zip(rows, inputs)
        ]
        for i, column in zip(rows, solved):
            wide = jnp.broadcast_to(column, (BLOCK, BLOCK))
            sums[i % SPAN] = wide
            out_ref[pl.ds(i, 1), :] = jnp.sum(
                jnp.where(eye, wide, 0.0), axis=0, keepdims=True
            )
        for i in rows:
            if g:
                over_row(i, functools.partial(pull, wide=sums[i % SPAN]), 0, True)


def sweep(rhs, factor):
    return pl.pallas_call(
        sweep_kernel,
        out_shape=jax.ShapeDtypeStruct((KTOP, BLOCK), jnp.float32),
        in_specs=[pl.BlockSpec(memory_space=pltpu.VMEM), pl.BlockSpec(memory_space=pl.ANY)],
        out_specs=pl.BlockSpec(memory_space=pltpu.VMEM),
        scratch_shapes=[
            pltpu.VMEM(factor.shape, jnp.float32),
            pltpu.VMEM((KTOP, 8, BLOCK), jnp.float32),
            pltpu.VMEM((KTOP, 8, BLOCK), jnp.float32),
            pltpu.VMEM((SPAN, BLOCK, BLOCK), jnp.float32),
            pltpu.SemaphoreType.DMA((KTOP, factor.shape[0] // KTOP)),
        ],
        compiler_params=pltpu.CompilerParams(vmem_limit_bytes=44 * 2**20),
    )(rhs, factor)


def split(value):
    high = value.astype(jnp.bfloat16)
    return high, (value - high.astype(jnp.float32)).astype(jnp.bfloat16)


def dot3(left, right):
    (a, b), (c, d) = left, right
    dot = functools.partial(jnp.dot, preferred_element_type=jnp.float32)
    both = dot(jnp.concatenate([a, b], axis=0), c)
    rows = a.shape[0]
    return both[:rows] + (dot(a, d) + both[rows:])


def prepare_kernel(*refs):
    outs = refs[len(refs) // 2 :]
    for ref, out in zip(refs, outs):
        for n in range(ref.shape[0]):
            high, low = split(ref[n].T)
            out[n, 0] = high
            out[n, 1] = low


def prepare(*matrices):
    return pl.pallas_call(
        prepare_kernel,
        out_shape=tuple(
            jax.ShapeDtypeStruct((m.shape[0], 2) + m.shape[1:], jnp.bfloat16) for m in matrices
        ),
    )(*matrices)


def finish_kernel(
    place_ref,
    near_ref,
    far_ref,
    root_panel_ref,
    mid_panel_ref,
    forward_root_ref,
    forward_mid_ref,
    forward_leaf_ref,
    root_inverse_ref,
    mid_inverse_ref,
    mid_coupling_ref,
    leaf_inverse_ref,
    leaf_coupling_ref,
    leaf_out,
    mid_out,
    root_out,
    top_out,
    acc,
):
    step = pl.program_id(0)
    half = near_ref.shape[0] // KTOP
    blocks = root_panel_ref.shape[0] // BLOCK
    mids = mid_panel_ref.shape[0]
    leaves = leaf_inverse_ref.shape[0]
    core = place_ref[1]

    def columns_of(block):
        return jnp.concatenate(
            [
                near_ref[pl.ds(block, half, stride=KTOP), :],
                far_ref[pl.ds(block, half, stride=KTOP), :],
            ],
            axis=0,
        )

    def ordered(value):
        return jnp.where(
            core == 0, value, jnp.concatenate([value[half:], value[:half]], axis=0)
        )

    @pl.when(step == 0)
    def _():
        acc[...] = jnp.zeros_like(acc)

    solved = split(
        jnp.concatenate([columns_of(step * blocks + t) for t in range(blocks)], axis=1)
    )
    panels = [root_panel_ref[...]] + [mid_panel_ref[m] for m in range(mids)]
    acc[...] += dot3(solved, split(jnp.concatenate(panels, axis=1)))

    @pl.when(step == pl.num_programs(0) - 1)
    def _():
        top_out[...] = ordered(columns_of(place_ref[0])).T
        pulls = [ordered(acc[:, n * BLOCK : (n + 1) * BLOCK]).T for n in range(1 + mids)]
        root = dot3((root_inverse_ref[0, 0], root_inverse_ref[0, 1]), split(forward_root_ref[...] - pulls[0]))
        root_out[...] = root
        root = split(root)
        for m in range(mids):
            term = dot3((mid_coupling_ref[m, 0], mid_coupling_ref[m, 1]), root)
            mid = dot3(
                (mid_inverse_ref[m, 0], mid_inverse_ref[m, 1]), split(forward_mid_ref[m] - term - pulls[1 + m])
            )
            mid_out[m] = mid
            mid = split(mid)
            for p in range(m * leaves // mids, (m + 1) * leaves // mids):
                term = dot3((leaf_coupling_ref[p, 0], leaf_coupling_ref[p, 1]), mid)
                leaf_out[p] = dot3(
                    (leaf_inverse_ref[p, 0], leaf_inverse_ref[p, 1]), split(forward_leaf_ref[p] - term)
                )


def finish(place, near, far, root_panel, mid_panel, *small):
    mids, leaves = mid_panel.shape[0], small[2].shape[0]
    steps = 2
    rows = KTOP * BLOCK // steps

    def whole(value):
        return pl.BlockSpec(value.shape, lambda t: (0,) * len(value.shape))

    out = functools.partial(jax.ShapeDtypeStruct, dtype=jnp.float32)
    shapes = (
        out((leaves, BLOCK, BLOCK)),
        out((mids, BLOCK, BLOCK)),
        out((BLOCK, BLOCK)),
        out((BLOCK, BLOCK)),
    )
    return pl.pallas_call(
        finish_kernel,
        grid=(steps,),
        out_shape=shapes,
        in_specs=[
            pl.BlockSpec(memory_space=pltpu.SMEM),
            whole(near),
            whole(far),
            pl.BlockSpec((rows, BLOCK), lambda t: (t, 0)),
            pl.BlockSpec((mids, rows, BLOCK), lambda t: (0, t, 0)),
        ]
        + [whole(value) for value in small],
        out_specs=tuple(whole(value) for value in shapes),
        scratch_shapes=[pltpu.VMEM((NRHS, (1 + mids) * BLOCK), jnp.float32)],
        compiler_params=pltpu.CompilerParams(vmem_limit_bytes=60 * 2**20),
    )(place, near, far, root_panel, mid_panel, *small)


def pack_kernel(
    pattern_ref, inverse_ref, factor_hbm, keep_ref, first_ref, second_ref, rows, turned, sem
):
    part = rows.shape[0]
    layer = lax.axis_index("layer")
    own_group = (lax.axis_index("chip") * 2 + lax.axis_index("core")) // SPAN
    top = pl.multiple_of(layer * part, part)
    copy = pltpu.make_async_copy(factor_hbm.at[pl.ds(top, part)], rows, sem)
    copy.start()
    turned[...] = inverse_ref[...].T
    keep_ref[KEEP] = turned[pl.ds(top, part), :]
    copy.wait()

    def weighted(j):
        weight = jnp.where(j // SPAN < own_group, pattern_ref[0, j], 0).astype(jnp.float32)
        return rows[:, pl.ds(pl.multiple_of(j * BLOCK, BLOCK), BLOCK)] * weight

    for j in range(KEEP):
        keep_ref[j] = weighted(j)
    for t in range(FIRST):
        first_ref[t] = weighted(KEEP + t)
    start = jnp.where(own_group == 7, 24, 16)
    for t in range(SECOND):
        second_ref[t] = weighted(start + t)


def merge_kernel(keep_hbm, first_ref, second_ref, out_hbm, sems):
    own_group = (lax.axis_index("chip") * 2 + lax.axis_index("core")) // SPAN
    for g in range(GROUPS // 2):
        second = SECOND if g % 2 == 0 else 0
        own, end = SPAN * g, KEEP - second

        @pl.when(own_group == g)
        def _():
            copies = [
                pltpu.make_async_copy(
                    first_ref.at[pl.ds(0, end - own)], out_hbm.at[pl.ds(own, end - own)], sems.at[0]
                )
            ]
            if second:
                copies.append(
                    pltpu.make_async_copy(second_ref, out_hbm.at[pl.ds(end, second)], sems.at[1])
                )
            for copy in copies:
                copy.start()
            for copy in copies:
                copy.wait()


def pack_rows(factor_row, pattern_row, inverse, layers):
    part = BLOCK // layers
    out = functools.partial(jax.ShapeDtypeStruct, dtype=jnp.float32)
    vmem = pl.BlockSpec(memory_space=pltpu.VMEM)
    params = pltpu.CompilerParams(vmem_limit_bytes=60 * 2**20)
    keep, first, second = pl.pallas_call(
        pack_kernel,
        out_shape=(
            out((SLOTS, part, BLOCK)),
            out((FIRST, part, BLOCK)),
            out((SECOND, part, BLOCK)),
        ),
        in_specs=[
            pl.BlockSpec(memory_space=pltpu.SMEM),
            vmem,
            pl.BlockSpec(memory_space=pl.ANY),
        ],
        out_specs=(vmem,) * 3,
        scratch_shapes=[
            pltpu.VMEM((part, KTOP * BLOCK), jnp.float32),
            pltpu.VMEM((BLOCK, BLOCK), jnp.float32),
            pltpu.SemaphoreType.DMA,
        ],
        compiler_params=params,
    )(pattern_row, inverse, factor_row)
    moves = ([], [])
    for g, parts in MOVED.items():
        for move, (_, _, device, _) in zip(moves, parts):
            move += [(i, device(i)) for i in range(SPAN * g, SPAN * (g + 1))]
    first = lax.ppermute(first, GRID, moves[0])
    second = lax.ppermute(second, GRID, moves[1])
    anywhere = pl.BlockSpec(memory_space=pl.ANY)
    return pl.pallas_call(
        merge_kernel,
        out_shape=out((SLOTS, part, BLOCK)),
        in_specs=[anywhere] + [vmem] * 2,
        out_specs=anywhere,
        scratch_shapes=[pltpu.SemaphoreType.DMA((2,))],
        input_output_aliases={0: 0},
    )(keep, first, second)


def swap_cores(value):
    return lax.ppermute(value, "core", [(0, 1), (1, 0)])


def local(
    leaf_inverse,
    leaf_coupling,
    leaf_rhs,
    mid_inverse,
    mid_coupling,
    mid_rhs,
    mid_top,
    root_inverse,
    root_top,
    root_rhs,
    top_inverse,
    top_factor,
    top_rhs,
    top_pattern,
):
    columns = leaf_rhs.shape[-1]
    half = columns // 2
    position = lax.axis_index(GRID)
    core = lax.axis_index("core")
    layer = lax.axis_index("layer")
    layers = lax.axis_size("layer")
    packed = pack_rows(top_factor[0], top_pattern, top_inverse[0], layers)
    factor = lax.all_gather(packed, ("layer",) + GRID, axis=0)

    leaf_inv = leaf_inverse[0, 0]
    leaf_links = leaf_coupling[0, 0]
    forward_leaf = product("pab,pbr->par", leaf_inv, leaf_rhs[0, 0])
    pulled = (
        product("pab,pbr->par", leaf_links, forward_leaf)
        .reshape(-1, 2, BLOCK, columns)
        .sum(axis=1)
    )
    forward_mid = product("mab,mbr->mar", mid_inverse[0, 0], mid_rhs[0, 0] - pulled)
    root_input = root_rhs[0, 0] - product("mab,mbr->ar", mid_coupling[0, 0], forward_mid)
    forward_root = product("ab,br->ar", root_inverse[0, 0], root_input)
    root_panel = root_top[0, 0]
    mid_panel = mid_top[0, 0]
    summed = product("br,kb->rk", forward_root, root_panel) + product(
        "mbr,mkb->rk", forward_mid, mid_panel
    )
    summed = summed.reshape(columns, KTOP, BLOCK)
    mine = ((jnp.arange(KTOP) == position) & (layer == 0))[None, :, None]
    summed = summed - jnp.where(mine, top_rhs[0].T[:, None, :], 0.0)
    prepared = prepare(
        root_inverse[0], mid_inverse[0, 0], mid_coupling[0, 0], leaf_inv, leaf_links
    )
    summed, prepared = lax.optimization_barrier((summed, prepared))
    away = lax.dynamic_slice_in_dim(summed, (1 - core) * half, half)
    home = lax.dynamic_slice_in_dim(summed, core * half, half)
    parts = lax.all_to_all(home + swap_cores(away), "layer", 0, 0, tiled=True)
    parts = parts.reshape(layers, half // layers, KTOP, BLOCK).sum(axis=0)
    residual = lax.all_to_all(parts, "chip", 0, 0, tiled=True).sum(axis=0)

    own_column = sweep(residual, factor)
    everywhere = jnp.broadcast_to(own_column[None], (half, KTOP, BLOCK))
    near = lax.all_to_all(everywhere, ("layer", "chip"), 0, 0, tiled=True)
    far = swap_cores(near)
    back_leaf, back_mid, back_root, own_top = finish(
        jnp.stack([position, core]).astype(jnp.int32),
        near.reshape(half * KTOP, BLOCK),
        far.reshape(half * KTOP, BLOCK),
        root_panel,
        mid_panel,
        forward_root,
        forward_mid,
        forward_leaf,
        *prepared,
    )
    return (back_leaf[None, None], back_mid[None, None], back_root[None, None], own_top[None])


def solution(mesh):
    layers, grid = mesh.devices.shape
    chips = Mesh(mesh.devices.reshape(layers, grid // 2, 2), ("layer",) + GRID)
    subtree = ("layer", GRID)
    placed = (
        P(*subtree, None, None, None),
        P(*subtree, None, None, None),
        P(*subtree, None, None, None),
        P(*subtree, None, None, None),
        P(*subtree, None, None, None),
        P(*subtree, None, None, None),
        P(*subtree, None, None, None),
        P(*subtree, None, None),
        P(*subtree, None, None),
        P(*subtree, None, None),
        P(GRID, None, None),
        P(GRID, None, None),
        P(GRID, None, None),
        P(GRID, None),
    )
    return jax.shard_map(
        local,
        mesh=chips,
        in_specs=placed,
        out_specs=(
            P(*subtree, None, None, None),
            P(*subtree, None, None, None),
            P(*subtree, None, None),
            P(GRID, None, None),
        ),
        check_vma=False,
    )
```
